256 devices in a mesh: walker: 16 (over x, y), param: 16 (over z, core).
Axes of the slice: x: 4, y: 4, z: 8, core: 2. Of those that a mesh axis runs over, the one named last changes fastest.
Arguments:
- occupation: int32 [16, 4096], P(None, 'walker'), may hold values from 0 to 1023
- inverse_slater: float32 [16, 16, 4096], P(None, None, 'walker'), may hold values from -1.5 to 1.5
- orbitals: float32 [1024, 512], replicated, may hold values from -6 to 6
- hop_orbitals: float32 [1024, 512], replicated, may hold values from -6 to 6
- local_energy: float32 [4096], P('walker'), may hold values from -6 to 6
- excitations: int32 [4, 65536], P(None, 'param'), may hold values from 0 to 511, as said below
- initial_block: float32 [65536, 8], P('param'), may hold values from -6 to 6
Outputs:
- basis_scaled: float32 [65536, 32], P('param')
- proj_h: float32 [32, 32], replicated
- proj_s: float32 [32, 32], replicated
The draws below stay inside these ranges and needn't reach their ends.
Inputs may be any that keep to these rules, and one draw needn't show every extreme that they name: `excitations`: rows 0 and 1 name two different electrons below 16; rows 2 and 3 name two different orbitals.
All inputs are finite; a program needn't handle non-finite values.
Results may differ from the reference program's by a relative error of at most 0.025.
Values may be sent and summed in bfloat16 or wider, within the bound.
No kernel may reach another device: no remote copies, remote signals or barrier semaphores. Data moves between devices by JAX's collectives and lax.ppermute only.
A program may use at most 128 MiB of HBM per device.

```python
import math
import jax
import jax.numpy as jnp
from jax import lax

NE = 16
NORB = 512
NSITE = 1024
PARAMS = 65536
NB = 8
ITERS = 3
WALKERS = 4096


def draw_excitations(key, part):
    keys = jax.random.split(key, 4)
    first = jax.random.randint(keys[0], (PARAMS,), 0, NE)
    second = (first + jax.random.randint(keys[1], (PARAMS,), 1, NE)) % NE
    orbital_one = jax.random.randint(keys[2], (PARAMS,), 0, NORB)
    orbital_two = (orbital_one + jax.random.randint(keys[3], (PARAMS,), 1, NORB)) % NORB
    return jnp.stack([first, second, orbital_one, orbital_two]).astype(jnp.int32)


def set_ends(drawn, rng, smallest, top_value):
    longest = drawn.shape.index(max(drawn.shape))
    spots = []
    for shift in (0, 1):
        where = [jax.random.randint(jax.random.fold_in(rng, axis), (), 0, length) for axis, length in enumerate(drawn.shape)]
        where[longest] = (where[longest] + shift) % drawn.shape[longest]
        spots.append(tuple(where))
    return drawn.at[spots[0]].set(smallest).at[spots[1]].set(top_value)


def block_levels(key, dims, cuts, low, top_value):
    loudness = 1.0
    for position, parts in cuts:
        heights = jax.random.uniform(jax.random.fold_in(jax.random.fold_in(key, 6), position), (parts,), jnp.float32, low / len(cuts), top_value / len(cuts))
        loudness = loudness * jnp.repeat(jnp.exp(heights), dims[position] // parts).reshape((-1,) + (1,) * (len(dims) - 1 - position))
    return loudness


def bell_draw(own_key, shape, spread, limit, cuts=(), held_as=jnp.bfloat16):
    level = block_levels(own_key, shape, cuts, -0.22, 0.18) if cuts else 1.0
    drawn = jax.random.normal(own_key, shape, jnp.float32) * spread * level
    return jnp.minimum(jnp.maximum(drawn, -limit), limit).astype(held_as)


def setup_inputs(seed: int = 0) -> dict:
    key_of = jax.random.split(jax.random.key(seed), 8)
    occupation = set_ends(jax.random.randint(key_of[0], (NE, WALKERS), 0, NSITE), jax.random.fold_in(key_of[0], 1), 0, NSITE - 1).astype(jnp.int32)
    inverse_slater = bell_draw(key_of[1], (NE, NE, WALKERS), NE ** -0.5, 1.5, ((2, 16),), jnp.float32)
    orbitals = bell_draw(key_of[2], (NSITE, NORB), 1.0, 6.0, (), jnp.float32)
    hop_orbitals = bell_draw(key_of[3], (NSITE, NORB), 1.0, 6.0, (), jnp.float32)
    local_energy = bell_draw(key_of[4], (WALKERS,), 1.0, 6.0, ((0, 16),), jnp.float32)
    excitations = draw_excitations(jax.random.fold_in(key_of[7], 71), 0)
    initial_block = bell_draw(key_of[6], (PARAMS, NB), 1.0, 6.0, ((0, 16),), jnp.float32)
    return dict(occupation=occupation, inverse_slater=inverse_slater, orbitals=orbitals, hop_orbitals=hop_orbitals, local_energy=local_energy, excitations=excitations, initial_block=initial_block)


EPS_SHIFT = 0.001
ENERGY_SHIFT = 0.5

def orthonormal(vectors, gram_matrix):
    lower_factor = jnp.linalg.cholesky(gram_matrix)
    return jax.scipy.linalg.solve_triangular(lower_factor, vectors.T, lower=True).T

def reference(occupation, inverse_slater, orbitals, hop_orbitals, local_energy, excitations, initial_block):
    highest = lax.Precision.HIGHEST
    walkers = local_energy.shape[0]
    orbital_rows = jnp.take(orbitals, occupation, axis=0)
    hopped_rows = jnp.take(hop_orbitals, occupation, axis=0)
    ratios = jnp.einsum('ikw,kwa->iaw', inverse_slater, orbital_rows, precision=highest).reshape(NE * NORB, walkers)
    energy_ratios = jnp.einsum('ikw,kwa->iaw', inverse_slater, hopped_rows, precision=highest).reshape(NE * NORB, walkers)
    param_blocks = 16
    block_size = PARAMS // param_blocks
    blocked = excitations.reshape(4, param_blocks, block_size).transpose(1, 0, 2)

    def pieces(table):
        first = table[0] * NORB + table[2]
        second = table[1] * NORB + table[3]
        cross_one = table[0] * NORB + table[3]
        cross_two = table[1] * NORB + table[2]
        return (first, second, cross_one, cross_two)

    def build_derivs(table):
        first, second, cross_one, cross_two = pieces(table)
        raw = jnp.take(ratios, first, axis=0) * jnp.take(ratios, second, axis=0) - jnp.take(ratios, cross_one, axis=0) * jnp.take(ratios, cross_two, axis=0)
        return raw

    def build_both(table):
        first, second, cross_one, cross_two = pieces(table)
        ratio_ia = jnp.take(ratios, first, axis=0)
        ratio_jb = jnp.take(ratios, second, axis=0)
        ratio_ib = jnp.take(ratios, cross_one, axis=0)
        ratio_ja = jnp.take(ratios, cross_two, axis=0)
        energy_ia = jnp.take(energy_ratios, first, axis=0)
        energy_jb = jnp.take(energy_ratios, second, axis=0)
        energy_ib = jnp.take(energy_ratios, cross_one, axis=0)
        energy_ja = jnp.take(energy_ratios, cross_two, axis=0)
        raw = ratio_ia * ratio_jb - ratio_ib * ratio_ja
        energy_raw = local_energy[None, :] * raw + energy_ia * ratio_jb + ratio_ia * energy_jb - energy_ib * ratio_ja - ratio_ib * energy_ja
        return (raw.astype(jnp.bfloat16), energy_raw.astype(jnp.bfloat16))

    def column_sums(table):
        derivs, energy_derivs = build_both(table)
        wide = derivs.astype(jnp.float32)
        return jnp.stack([lax.optimization_barrier(jnp.sum(wide, axis=1)), lax.optimization_barrier(jnp.sum(wide * wide, axis=1)), lax.optimization_barrier(jnp.sum(energy_derivs.astype(jnp.float32), axis=1))])
    sums = lax.map(column_sums, blocked).transpose(1, 0, 2).reshape(3, PARAMS)
    mean_o = sums[0] / walkers
    mean_h = sums[2] / walkers
    s_diagonal = sums[1] / walkers - mean_o * mean_o + EPS_SHIFT

    def apply_operators(block):
        block_b = block.astype(jnp.bfloat16)
        pieces_b = block_b.reshape(param_blocks, block_size, NB)

        def forward(totals, item):
            table, piece = item
            derivs, energy_derivs = build_both(table)
            term = jnp.concatenate([jnp.dot(derivs.T.astype(jnp.float32), piece.astype(jnp.float32), preferred_element_type=jnp.float32), jnp.dot(energy_derivs.T.astype(jnp.float32), piece.astype(jnp.float32), preferred_element_type=jnp.float32)], axis=1)
            return (totals + term, None)
        totals, unused = lax.scan(forward, jnp.zeros((walkers, 2 * NB), jnp.float32), (blocked, pieces_b))
        block_wide = block_b.astype(jnp.float32)
        centering = jnp.concatenate([jnp.dot(mean_o, block_wide, precision=highest), jnp.dot(mean_h, block_wide, precision=highest)])
        row_images = (totals - centering[None, :]).astype(jnp.bfloat16)

        def backward(table):
            derivs = build_derivs(table).astype(jnp.bfloat16)
            return jnp.dot(derivs.astype(jnp.float32), row_images.astype(jnp.float32), preferred_element_type=jnp.float32)
        images = lax.map(backward, blocked).reshape(PARAMS, 2 * NB)
        s_image = images[:, :NB] / walkers + EPS_SHIFT * block
        h_image = images[:, NB:] / walkers + ENERGY_SHIFT * block
        return (s_image, h_image)
    block = orthonormal(initial_block, jnp.dot(initial_block.T, initial_block, precision=highest))
    basis_list = []
    s_images = []
    h_images = []
    for iteration in range(ITERS + 1):
        s_image, h_image = apply_operators(block)
        basis_list.append(block)
        s_images.append(s_image)
        h_images.append(h_image)
        if iteration < ITERS:
            a_matrix = jnp.dot(block.T, s_image, precision=highest)
            b_matrix = jnp.dot(block.T, h_image, precision=highest)
            rayleigh = jax.scipy.linalg.cho_solve((jnp.linalg.cholesky(a_matrix), True), b_matrix)
            residual = h_image - jnp.dot(s_image, rayleigh, precision=highest)
            correction = residual / s_diagonal[:, None]
            earlier = jnp.concatenate(basis_list, axis=1)
            correlation = jnp.dot(earlier.T, correction, precision=highest)
            correction = correction - jnp.dot(earlier, correlation, precision=highest)
            block = orthonormal(correction, jnp.dot(correction.T, correction, precision=highest))
    whole_basis = jnp.concatenate(basis_list, axis=1)
    proj_h = jnp.dot(whole_basis.T, jnp.concatenate(h_images, axis=1), precision=highest)
    proj_s = jnp.dot(whole_basis.T, jnp.concatenate(s_images, axis=1), precision=highest)
    return (math.sqrt(PARAMS) * whole_basis, proj_h, proj_s)
```

```python
import math

import jax
import jax.numpy as jnp
from jax import lax
from jax.sharding import PartitionSpec as P

ITERS = 3
EPS_SHIFT = 0.001
ENERGY_SHIFT = 0.5
HIGHEST = lax.Precision.HIGHEST


def dot_nt(left, right):
    return lax.dot_general(
        left, right, (((1,), (1,)), ((), ())), precision=HIGHEST, preferred_element_type=jnp.float32
    )


def dot_nn(left, right):
    return jnp.dot(left, right, precision=HIGHEST, preferred_element_type=jnp.float32)


def exchange(parts, axis):
    return lax.all_to_all(lax.optimization_barrier(parts), axis, 0, 0)


def to_all(value, axis):
    copies = jnp.broadcast_to(value[None], (lax.axis_size(axis),) + value.shape)
    return exchange(copies, axis)


def by_owner(values, owners):
    rows = values.shape[0]
    return values.reshape(rows, owners, -1).transpose(1, 0, 2)


def pad_columns(values, columns):
    return jnp.pad(values, ((0, 0), (0, columns - values.shape[1])))


def split_in_two(values):
    high = lax.reduce_precision(values, exponent_bits=8, mantissa_bits=7)
    return jnp.concatenate([high, values - high]).astype(jnp.bfloat16)


def forward(vectors, derivs, energy_derivs):
    count = vectors.shape[0]
    halves = split_in_two(vectors)
    images = []
    for table in (derivs, energy_derivs):
        both = jnp.dot(halves, table, preferred_element_type=jnp.float32)
        images.append(both[:count] + both[count:])
    return jnp.concatenate(images)


def build(occupation, inverse_slater, orbitals, hop_orbitals, local_energy, excitations):
    orbital_count = orbitals.shape[1]
    electrons = occupation.shape[0]
    local_walkers = local_energy.shape[0]
    orbital_rows = jnp.take(orbitals, occupation, axis=0)
    hopped_rows = jnp.take(hop_orbitals, occupation, axis=0)
    ratios = jnp.einsum("ikw,kwa->iaw", inverse_slater, orbital_rows, precision=HIGHEST).reshape(
        electrons * orbital_count, local_walkers
    )
    energy_ratios = jnp.einsum(
        "ikw,kwa->iaw", inverse_slater, hopped_rows, precision=HIGHEST
    ).reshape(electrons * orbital_count, local_walkers)
    first = excitations[0] * orbital_count + excitations[2]
    second = excitations[1] * orbital_count + excitations[3]
    cross_one = excitations[0] * orbital_count + excitations[3]
    cross_two = excitations[1] * orbital_count + excitations[2]
    ratio_ia = jnp.take(ratios, first, axis=0)
    ratio_jb = jnp.take(ratios, second, axis=0)
    ratio_ib = jnp.take(ratios, cross_one, axis=0)
    ratio_ja = jnp.take(ratios, cross_two, axis=0)
    energy_ia = jnp.take(energy_ratios, first, axis=0)
    energy_jb = jnp.take(energy_ratios, second, axis=0)
    energy_ib = jnp.take(energy_ratios, cross_one, axis=0)
    energy_ja = jnp.take(energy_ratios, cross_two, axis=0)
    raw = ratio_ia * ratio_jb - ratio_ib * ratio_ja
    energy_raw = (
        local_energy[None, :] * raw
        + energy_ia * ratio_jb
        + ratio_ia * energy_jb
        - energy_ib * ratio_ja
        - ratio_ib * energy_ja
    )
    derivs = raw.astype(jnp.bfloat16)
    energy_derivs = energy_raw.astype(jnp.bfloat16)
    wide = derivs.astype(jnp.float32)
    sums = jnp.stack(
        [
            jnp.sum(wide, axis=1),
            jnp.sum(wide * wide, axis=1),
            jnp.sum(energy_derivs.astype(jnp.float32), axis=1),
        ]
    )
    return derivs, energy_derivs, sums


def inverse_factor(gram):
    lower_factor = jnp.linalg.cholesky(gram)
    return jax.scipy.linalg.solve_triangular(
        lower_factor, jnp.eye(gram.shape[0], dtype=gram.dtype), lower=True
    )


def on_device(
    occupation, inverse_slater, orbitals, hop_orbitals, local_energy, excitations, initial_block
):
    walker_devices = lax.axis_size("walker")
    local_walkers = local_energy.shape[0]
    walkers = local_walkers * walker_devices
    block_rows = excitations.shape[1]
    count = initial_block.shape[1]
    params = block_rows * lax.axis_size("param")
    owned = block_rows // walker_devices
    derivs, energy_derivs, sums = build(
        occupation, inverse_slater, orbitals, hop_orbitals, local_energy, excitations
    )
    start = initial_block.T

    def across_params(images, grams):
        sent = jnp.concatenate([images, pad_columns(grams, local_walkers)])
        total = jnp.sum(to_all(sent, "param"), axis=0)
        return total[: 2 * count], total[2 * count :, : grams.shape[1]]

    images, gram = across_params(
        forward(start, derivs, energy_derivs), dot_nt(start, start)
    )
    factor = inverse_factor(gram)
    totals = jnp.concatenate([dot_nn(factor, images[:count]), dot_nn(factor, images[count:])])
    center_part = jnp.sum(totals, axis=1)
    sent = jnp.concatenate(
        [
            by_owner(sums, walker_devices),
            jnp.broadcast_to(
                jnp.pad(center_part, (0, owned - 2 * count))[None, None], (walker_devices, 1, owned)
            ),
        ],
        axis=1,
    )
    total = jnp.sum(exchange(sent, "walker"), axis=0) / walkers
    means = jnp.stack([total[0], total[2]])
    s_diagonal = total[1] - total[0] * total[0] + EPS_SHIFT
    center = total[3, : 2 * count]

    offset = lax.axis_index("walker") * owned
    block = dot_nn(factor, lax.dynamic_slice_in_dim(start, offset, owned, 1))
    whole = [dot_nn(factor, start)]
    basis = [block]
    all_totals = [totals]
    all_centers = [center]
    all_rows = []
    for iteration in range(ITERS + 1):
        row_images = (totals - center[:, None]).astype(jnp.bfloat16)
        all_rows.append(row_images)
        if iteration == ITERS:
            break
        back = lax.dot_general(
            row_images, derivs, (((1,), (1,)), ((), ())), preferred_element_type=jnp.float32
        )
        inner = lax.dot_general(
            totals[:count],
            row_images.astype(jnp.float32),
            (((1,), (1,)), ((), ())),
            precision=HIGHEST,
        )
        sent = jnp.concatenate(
            [
                by_owner(back, walker_devices),
                jnp.broadcast_to(
                    pad_columns(inner, owned)[None], (walker_devices, count, owned)
                ),
            ],
            axis=1,
        )
        total = jnp.sum(exchange(sent, "walker"), axis=0) / walkers
        inner = total[2 * count :, : 2 * count]
        a_matrix = inner[:, :count] + EPS_SHIFT * jnp.eye(count)
        b_matrix = inner[:, count:] + ENERGY_SHIFT * jnp.eye(count)
        s_image = total[:count] + EPS_SHIFT * block
        h_image = total[count : 2 * count] + ENERGY_SHIFT * block
        rayleigh = jax.scipy.linalg.cho_solve((jnp.linalg.cholesky(a_matrix), True), b_matrix)
        correction = (h_image - dot_nn(rayleigh.T, s_image)) / s_diagonal[None]
        grams = dot_nt(correction, jnp.concatenate(basis + [correction, means]))
        got = to_all(
            jnp.concatenate([correction, pad_columns(grams, 128)], axis=1), "walker"
        )
        grams = jnp.sum(got[:, :, owned : owned + grams.shape[1]], axis=0)
        whole_correction = got[:, :, :owned].transpose(1, 0, 2).reshape(count, block_rows)
        images, grams = across_params(
            forward(whole_correction, derivs, energy_derivs), grams
        )
        earlier = count * (iteration + 1)
        overlap = grams[:, :earlier]
        gram = grams[:, earlier : earlier + count] - dot_nt(overlap, overlap)
        factor = inverse_factor(gram)

        def advance(new, old):
            return dot_nn(factor, new - dot_nn(overlap, old))

        block = advance(correction, jnp.concatenate(basis))
        whole.append(advance(whole_correction, jnp.concatenate(whole)))
        totals = jnp.concatenate(
            [
                advance(images[:count], jnp.concatenate([t[:count] for t in all_totals])),
                advance(images[count:], jnp.concatenate([t[count:] for t in all_totals])),
            ]
        )
        center = jnp.concatenate(
            [
                advance(
                    grams[:, earlier + count + part : earlier + count + part + 1],
                    jnp.concatenate([c[part * count : (part + 1) * count] for c in all_centers])[
                        :, None
                    ],
                )[:, 0]
                for part in range(2)
            ]
        )
        basis.append(block)
        all_totals.append(totals)
        all_centers.append(center)
    lefts = jnp.concatenate([t[:count] for t in all_totals])
    rights = jnp.concatenate(
        [r[:count] for r in all_rows] + [r[count:] for r in all_rows]
    ).astype(jnp.float32)
    proj = jnp.sum(to_all(dot_nt(lefts, rights), "walker"), axis=0) / walkers
    size = lefts.shape[0]
    proj_s = proj[:, :size] + EPS_SHIFT * jnp.eye(size)
    proj_h = proj[:, size:] + ENERGY_SHIFT * jnp.eye(size)
    return (math.sqrt(params) * jnp.concatenate(whole).T, proj_h, proj_s)


def solution(mesh):
    placed = (
        P(None, "walker"),
        P(None, None, "walker"),
        P(),
        P(),
        P("walker"),
        P(None, "param"),
        P("param", None),
    )
    return jax.shard_map(
        on_device,
        mesh=mesh,
        in_specs=placed,
        out_specs=(P("param", None), P(), P()),
        check_vma=False,
    )
```

```python
import math

import jax
import jax.numpy as jnp
from jax import lax
from jax.experimental import pallas as pl
from jax.experimental.pallas import tpu as pltpu
from jax.sharding import PartitionSpec as P

ITERS = 3
EPS_SHIFT = 0.001
ENERGY_SHIFT = 0.5
HIGHEST = lax.Precision.HIGHEST


def dot_nt(left, right):
    return lax.dot_general(
        left, right, (((1,), (1,)), ((), ())), precision=HIGHEST, preferred_element_type=jnp.float32
    )


def dot_nn(left, right):
    return jnp.dot(left, right, precision=HIGHEST, preferred_element_type=jnp.float32)


def exchange(parts, axis):
    return lax.all_to_all(lax.optimization_barrier(parts), axis, 0, 0)


def to_all(value, axis):
    copies = jnp.broadcast_to(value[None], (lax.axis_size(axis),) + value.shape)
    return exchange(copies, axis)


def by_owner(values, owners):
    rows = values.shape[0]
    return values.reshape(rows, owners, -1).transpose(1, 0, 2)


def pad_columns(values, columns):
    return jnp.pad(values, ((0, 0), (0, columns - values.shape[1])))


def split_in_two(values):
    high = lax.reduce_precision(values, exponent_bits=8, mantissa_bits=7)
    return jnp.concatenate([high, values - high]).astype(jnp.bfloat16)


def forward(vectors, derivs, energy_derivs):
    count = vectors.shape[0]
    halves = split_in_two(vectors)
    images = []
    for table in (derivs, energy_derivs):
        both = jnp.dot(halves, table, preferred_element_type=jnp.float32)
        images.append(both[:count] + both[count:])
    return jnp.concatenate(images)


LANES = 128
ROWS = 8
GROUP = 64


def build_kernel(
    place_ref, occupation_ref, inverse_ref, orbitals_ref, hop_ref, energy_ref,
    derivs_ref, energy_derivs_ref,
    high_ref, low_ref, sites_ref, rows_ref, wide_ref, table_ref, first_ref, second_ref,
):
    electrons, walkers = occupation_ref.shape
    sites, orbitals = orbitals_ref.shape
    params = derivs_ref.shape[0]
    halves = walkers // LANES
    tiles = orbitals // ROWS

    for half in range(halves):
        for row in range(electrons * electrons):
            wide_ref[half, row] = jnp.broadcast_to(
                inverse_ref[row : row + 1, half * LANES : (half + 1) * LANES], (ROWS, LANES)
            )
    for number, source in enumerate((orbitals_ref, hop_ref)):
        for column in range(0, orbitals, LANES):
            turned = source[:, column : column + LANES].T
            high = turned.astype(jnp.bfloat16)
            where = pl.ds(number * orbitals + column, LANES)
            high_ref[where, :] = high
            low_ref[where, :] = (turned - high.astype(jnp.float32)).astype(jnp.bfloat16)

    def pick(electron, carry):
        occupied = occupation_ref[pl.ds(electron, 1), :]
        index = lax.broadcasted_iota(jnp.int32, (sites, walkers), 0)
        sites_ref[...] = jnp.where(index == occupied, 1.0, 0.0).astype(jnp.bfloat16)
        for row in range(0, 2 * orbitals, 256):
            where = pl.ds(row, 256)
            rows_ref[electron, where, :] = jnp.dot(
                high_ref[where, :], sites_ref[...], preferred_element_type=jnp.float32
            ) + jnp.dot(low_ref[where, :], sites_ref[...], preferred_element_type=jnp.float32)
        return carry

    lax.fori_loop(0, electrons, pick, 0)

    def contract(tile, carry):
        for half in range(halves):
            lanes = slice(half * LANES, (half + 1) * LANES)
            plain = [rows_ref[k, pl.ds(pl.multiple_of(tile * ROWS, ROWS), ROWS), lanes] for k in range(electrons)]
            hopped = [
                rows_ref[k, pl.ds(pl.multiple_of(orbitals + tile * ROWS, ROWS), ROWS), lanes]
                for k in range(electrons)
            ]
            scale = energy_ref[0:1, lanes] * 0.5
            for i in range(electrons):
                weight = wide_ref[half, i * electrons]
                ratio = weight * plain[0]
                energy = weight * hopped[0]
                for k in range(1, electrons):
                    weight = wide_ref[half, i * electrons + k]
                    ratio += weight * plain[k]
                    energy += weight * hopped[k]
                base = pl.multiple_of((i * tiles + tile) * 4 * ROWS, ROWS)
                table_ref[pl.ds(base + half, ROWS, stride=4), :] = ratio
                table_ref[pl.ds(base + 2 + half, ROWS, stride=4), :] = energy + scale * ratio
        return carry

    lax.fori_loop(0, tiles, contract, 0)

    def pairs(group, carry):
        for j in range(GROUP):

            def take(which, part):
                return table_ref[pl.ds(pl.multiple_of(place_ref[which * params + group * GROUP + j], 4) + part * 2, 2), :]

            ia, jb, ib, ja = (take(which, 0) for which in range(4))
            e_ia, e_jb, e_ib, e_ja = (take(which, 1) for which in range(4))
            spot = pl.ds(2 * j, 2)
            first_ref[spot, :] = ia * jb - ib * ja
            second_ref[spot, :] = (e_ia * jb + ia * e_jb) - (e_ib * ja + ib * e_ja)
        for source, target in ((first_ref, derivs_ref), (second_ref, energy_derivs_ref)):
            for row in range(0, GROUP, 2 * ROWS):
                for half in range(2):
                    target[
                        pl.ds(pl.multiple_of(group * GROUP + row, 2 * ROWS), 2 * ROWS),
                        half * LANES : (half + 1) * LANES,
                    ] = source[pl.ds(row * 2 + half, 2 * ROWS, stride=2), :].astype(jnp.bfloat16)
        return carry

    lax.fori_loop(0, params // GROUP, pairs, 0)


def build(occupation, inverse_slater, orbitals, hop_orbitals, local_energy, excitations):
    electrons, walkers = occupation.shape
    sites, orbital_count = orbitals.shape
    params = excitations.shape[1]

    def place(electron, orbital):
        row = electron * orbital_count + orbital
        return row * 4

    i, j, a, b = excitations
    places = jnp.concatenate([place(i, a), place(j, b), place(i, b), place(j, a)])
    vmem = pl.BlockSpec(memory_space=pltpu.VMEM)
    derivs, energy_derivs = pl.pallas_call(
        build_kernel,
        out_shape=[jax.ShapeDtypeStruct((params, walkers), jnp.bfloat16)] * 2,
        in_specs=[pl.BlockSpec(memory_space=pltpu.SMEM)] + [vmem] * 5,
        out_specs=[vmem] * 2,
        scratch_shapes=[
            pltpu.VMEM((2 * orbital_count, sites), jnp.bfloat16),
            pltpu.VMEM((2 * orbital_count, sites), jnp.bfloat16),
            pltpu.VMEM((sites, walkers), jnp.bfloat16),
            pltpu.VMEM((electrons, 2 * orbital_count, walkers), jnp.float32),
            pltpu.VMEM((walkers // LANES, electrons * electrons, ROWS, LANES), jnp.float32),
            pltpu.VMEM((electrons * orbital_count * 4, LANES), jnp.float32),
            pltpu.VMEM((GROUP * 2, LANES), jnp.float32),
            pltpu.VMEM((GROUP * 2, LANES), jnp.float32),
        ],
        compiler_params=pltpu.CompilerParams(vmem_limit_bytes=60 * 1024 * 1024),
    )(
        places,
        occupation,
        inverse_slater.reshape(electrons * electrons, walkers),
        orbitals,
        hop_orbitals,
        local_energy[None],
    )
    wide = derivs.astype(jnp.float32)
    sums = jnp.stack(
        [
            jnp.sum(wide, axis=1),
            jnp.sum(wide * wide, axis=1),
            jnp.sum(energy_derivs.astype(jnp.float32), axis=1),
        ]
    )
    return derivs, energy_derivs, sums


def inverse_factor(gram):
    lower_factor = jnp.linalg.cholesky(gram)
    return jax.scipy.linalg.solve_triangular(
        lower_factor, jnp.eye(gram.shape[0], dtype=gram.dtype), lower=True
    )


def on_device(
    occupation, inverse_slater, orbitals, hop_orbitals, local_energy, excitations, initial_block
):
    walker_devices = lax.axis_size("walker")
    local_walkers = local_energy.shape[0]
    walkers = local_walkers * walker_devices
    block_rows = excitations.shape[1]
    count = initial_block.shape[1]
    params = block_rows * lax.axis_size("param")
    owned = block_rows // walker_devices
    derivs, energy_derivs, sums = build(
        occupation, inverse_slater, orbitals, hop_orbitals, local_energy, excitations
    )
    start = initial_block.T

    def across_params(images, grams):
        sent = jnp.concatenate([images, pad_columns(grams, local_walkers)])
        total = jnp.sum(to_all(sent, "param"), axis=0)
        return total[: 2 * count], total[2 * count :, : grams.shape[1]]

    images, gram = across_params(
        forward(start, derivs, energy_derivs), dot_nt(start, start)
    )
    factor = inverse_factor(gram)
    totals = jnp.concatenate([dot_nn(factor, images[:count]), dot_nn(factor, images[count:])])
    center_part = jnp.sum(totals, axis=1)
    sent = jnp.concatenate(
        [
            by_owner(sums, walker_devices),
            jnp.broadcast_to(
                jnp.pad(center_part, (0, owned - 2 * count))[None, None], (walker_devices, 1, owned)
            ),
        ],
        axis=1,
    )
    total = jnp.sum(exchange(sent, "walker"), axis=0) / walkers
    means = jnp.stack([total[0], total[2]])
    s_diagonal = total[1] - total[0] * total[0] + EPS_SHIFT
    center = total[3, : 2 * count]

    offset = lax.axis_index("walker") * owned
    block = dot_nn(factor, lax.dynamic_slice_in_dim(start, offset, owned, 1))
    whole = [dot_nn(factor, start)]
    basis = [block]
    all_totals = [totals]
    all_centers = [center]
    all_rows = []
    for iteration in range(ITERS + 1):
        row_images = (totals - center[:, None]).astype(jnp.bfloat16)
        all_rows.append(row_images)
        if iteration == ITERS:
            break
        back = lax.dot_general(
            row_images, derivs, (((1,), (1,)), ((), ())), preferred_element_type=jnp.float32
        )
        inner = lax.dot_general(
            totals[:count],
            row_images.astype(jnp.float32),
            (((1,), (1,)), ((), ())),
            precision=HIGHEST,
        )
        sent = jnp.concatenate(
            [
                by_owner(back, walker_devices),
                jnp.broadcast_to(
                    pad_columns(inner, owned)[None], (walker_devices, count, owned)
                ),
            ],
            axis=1,
        )
        total = jnp.sum(exchange(sent, "walker"), axis=0) / walkers
        inner = total[2 * count :, : 2 * count]
        a_matrix = inner[:, :count] + EPS_SHIFT * jnp.eye(count)
        b_matrix = inner[:, count:] + ENERGY_SHIFT * jnp.eye(count)
        s_image = total[:count] + EPS_SHIFT * block
        h_image = total[count : 2 * count] + ENERGY_SHIFT * block
        rayleigh = jax.scipy.linalg.cho_solve((jnp.linalg.cholesky(a_matrix), True), b_matrix)
        correction = (h_image - dot_nn(rayleigh.T, s_image)) / s_diagonal[None]
        grams = dot_nt(correction, jnp.concatenate(basis + [correction, means]))
        got = to_all(
            jnp.concatenate([correction, pad_columns(grams, 128)], axis=1), "walker"
        )
        grams = jnp.sum(got[:, :, owned : owned + grams.shape[1]], axis=0)
        whole_correction = got[:, :, :owned].transpose(1, 0, 2).reshape(count, block_rows)
        images, grams = across_params(
            forward(whole_correction, derivs, energy_derivs), grams
        )
        earlier = count * (iteration + 1)
        overlap = grams[:, :earlier]
        gram = grams[:, earlier : earlier + count] - dot_nt(overlap, overlap)
        factor = inverse_factor(gram)

        def advance(new, old):
            return dot_nn(factor, new - dot_nn(overlap, old))

        block = advance(correction, jnp.concatenate(basis))
        whole.append(advance(whole_correction, jnp.concatenate(whole)))
        totals = jnp.concatenate(
            [
                advance(images[:count], jnp.concatenate([t[:count] for t in all_totals])),
                advance(images[count:], jnp.concatenate([t[count:] for t in all_totals])),
            ]
        )
        center = jnp.concatenate(
            [
                advance(
                    grams[:, earlier + count + part : earlier + count + part + 1],
                    jnp.concatenate([c[part * count : (part + 1) * count] for c in all_centers])[
                        :, None
                    ],
                )[:, 0]
                for part in range(2)
            ]
        )
        basis.append(block)
        all_totals.append(totals)
        all_centers.append(center)
    lefts = jnp.concatenate([t[:count] for t in all_totals])
    rights = jnp.concatenate(
        [r[:count] for r in all_rows] + [r[count:] for r in all_rows]
    ).astype(jnp.float32)
    proj = jnp.sum(to_all(dot_nt(lefts, rights), "walker"), axis=0) / walkers
    size = lefts.shape[0]
    proj_s = proj[:, :size] + EPS_SHIFT * jnp.eye(size)
    proj_h = proj[:, size:] + ENERGY_SHIFT * jnp.eye(size)
    return (math.sqrt(params) * jnp.concatenate(whole).T, proj_h, proj_s)


def solution(mesh):
    placed = (
        P(None, "walker"),
        P(None, None, "walker"),
        P(),
        P(),
        P("walker"),
        P(None, "param"),
        P("param", None),
    )
    return jax.shard_map(
        on_device,
        mesh=mesh,
        in_specs=placed,
        out_specs=(P("param", None), P(), P()),
        check_vma=False,
    )
```

```python
import math

import jax
import jax.numpy as jnp
from jax import lax
from jax.experimental import pallas as pl
from jax.experimental.pallas import tpu as pltpu
from jax.sharding import PartitionSpec as P

ITERS = 3
EPS_SHIFT = 0.001
ENERGY_SHIFT = 0.5
HIGHEST = lax.Precision.HIGHEST


def dot_nt(left, right):
    return lax.dot_general(
        left, right, (((1,), (1,)), ((), ())), precision=HIGHEST, preferred_element_type=jnp.float32
    )


def dot_nn(left, right):
    return jnp.dot(left, right, precision=HIGHEST, preferred_element_type=jnp.float32)


def exchange(parts, axis):
    return lax.all_to_all(lax.optimization_barrier(parts), axis, 0, 0)


def to_all(value, axis):
    copies = jnp.broadcast_to(value[None], (lax.axis_size(axis),) + value.shape)
    return exchange(copies, axis)


def by_owner(values, owners):
    rows = values.shape[0]
    return values.reshape(rows, owners, -1).transpose(1, 0, 2)


def pad_columns(values, columns):
    return jnp.pad(values, ((0, 0), (0, columns - values.shape[1])))


def split_in_two(values):
    high = lax.reduce_precision(values, exponent_bits=8, mantissa_bits=7)
    return jnp.concatenate([high, values - high]).astype(jnp.bfloat16)


def split_in_three(values):
    high = lax.reduce_precision(values, exponent_bits=8, mantissa_bits=7)
    rest = values - high
    middle = lax.reduce_precision(rest, exponent_bits=8, mantissa_bits=7)
    return jnp.concatenate([high, middle, rest - middle], axis=1).astype(jnp.bfloat16)


def joined(thirds, columns):
    return thirds[:, :columns] + thirds[:, columns : 2 * columns] + thirds[:, 2 * columns : 3 * columns]


def forward(vectors, derivs, energy_derivs):
    count = vectors.shape[0]
    halves = split_in_two(vectors)
    images = []
    for table in (derivs, energy_derivs):
        both = jnp.dot(halves, table, preferred_element_type=jnp.float32)
        images.append(both[:count] + both[count:])
    return jnp.concatenate(images)


LANES = 128
ROWS = 8
GROUP = 64


def build_kernel(
    place_ref, occupation_ref, inverse_ref, orbitals_ref, hop_ref, energy_ref,
    derivs_ref, energy_derivs_ref,
    high_ref, low_ref, sites_ref, rows_ref, wide_ref, table_ref, first_ref, second_ref,
):
    electrons, walkers = occupation_ref.shape
    sites, orbitals = orbitals_ref.shape
    params = derivs_ref.shape[0]
    halves = walkers // LANES
    tiles = orbitals // ROWS

    for half in range(halves):
        for row in range(electrons * electrons):
            wide_ref[half, row] = jnp.broadcast_to(
                inverse_ref[row : row + 1, half * LANES : (half + 1) * LANES], (ROWS, LANES)
            )
    for number, source in enumerate((orbitals_ref, hop_ref)):
        for column in range(0, orbitals, LANES):
            turned = source[:, column : column + LANES].T
            high = turned.astype(jnp.bfloat16)
            where = pl.ds(number * orbitals + column, LANES)
            high_ref[where, :] = high
            low_ref[where, :] = (turned - high.astype(jnp.float32)).astype(jnp.bfloat16)

    def pick(electron, carry):
        occupied = occupation_ref[pl.ds(electron, 1), :]
        index = lax.broadcasted_iota(jnp.int32, (sites, walkers), 0)
        sites_ref[...] = jnp.where(index == occupied, 1.0, 0.0).astype(jnp.bfloat16)
        for row in range(0, 2 * orbitals, 256):
            where = pl.ds(row, 256)
            rows_ref[electron, where, :] = jnp.dot(
                high_ref[where, :], sites_ref[...], preferred_element_type=jnp.float32
            ) + jnp.dot(low_ref[where, :], sites_ref[...], preferred_element_type=jnp.float32)
        return carry

    lax.fori_loop(0, electrons, pick, 0)

    def contract(tile, carry):
        for half in range(halves):
            lanes = slice(half * LANES, (half + 1) * LANES)
            plain = [rows_ref[k, pl.ds(pl.multiple_of(tile * ROWS, ROWS), ROWS), lanes] for k in range(electrons)]
            hopped = [
                rows_ref[k, pl.ds(pl.multiple_of(orbitals + tile * ROWS, ROWS), ROWS), lanes]
                for k in range(electrons)
            ]
            scale = energy_ref[0:1, lanes] * 0.5
            for i in range(electrons):
                weight = wide_ref[half, i * electrons]
                ratio = weight * plain[0]
                energy = weight * hopped[0]
                for k in range(1, electrons):
                    weight = wide_ref[half, i * electrons + k]
                    ratio += weight * plain[k]
                    energy += weight * hopped[k]
                base = pl.multiple_of((i * tiles + tile) * 4 * ROWS, ROWS)
                table_ref[pl.ds(base + half, ROWS, stride=4), :] = ratio
                table_ref[pl.ds(base + 2 + half, ROWS, stride=4), :] = energy + scale * ratio
        return carry

    lax.fori_loop(0, tiles, contract, 0)

    def pairs(group, carry):
        for j in range(GROUP):

            def take(which, part):
                return table_ref[pl.ds(pl.multiple_of(place_ref[which * params + group * GROUP + j], 4) + part * 2, 2), :]

            ia, jb, ib, ja = (take(which, 0) for which in range(4))
            e_ia, e_jb, e_ib, e_ja = (take(which, 1) for which in range(4))
            spot = pl.ds(2 * j, 2)
            first_ref[spot, :] = ia * jb - ib * ja
            second_ref[spot, :] = (e_ia * jb + ia * e_jb) - (e_ib * ja + ib * e_ja)
        for source, target in ((first_ref, derivs_ref), (second_ref, energy_derivs_ref)):
            for row in range(0, GROUP, 2 * ROWS):
                for half in range(2):
                    target[
                        pl.ds(pl.multiple_of(group * GROUP + row, 2 * ROWS), 2 * ROWS),
                        half * LANES : (half + 1) * LANES,
                    ] = source[pl.ds(row * 2 + half, 2 * ROWS, stride=2), :].astype(jnp.bfloat16)
        return carry

    lax.fori_loop(0, params // GROUP, pairs, 0)


def build(occupation, inverse_slater, orbitals, hop_orbitals, local_energy, excitations):
    electrons, walkers = occupation.shape
    sites, orbital_count = orbitals.shape
    params = excitations.shape[1]

    def place(electron, orbital):
        row = electron * orbital_count + orbital
        return row * 4

    i, j, a, b = excitations
    places = jnp.concatenate([place(i, a), place(j, b), place(i, b), place(j, a)])
    vmem = pl.BlockSpec(memory_space=pltpu.VMEM)
    derivs, energy_derivs = pl.pallas_call(
        build_kernel,
        out_shape=[jax.ShapeDtypeStruct((params, walkers), jnp.bfloat16)] * 2,
        in_specs=[pl.BlockSpec(memory_space=pltpu.SMEM)] + [vmem] * 5,
        out_specs=[vmem] * 2,
        scratch_shapes=[
            pltpu.VMEM((2 * orbital_count, sites), jnp.bfloat16),
            pltpu.VMEM((2 * orbital_count, sites), jnp.bfloat16),
            pltpu.VMEM((sites, walkers), jnp.bfloat16),
            pltpu.VMEM((electrons, 2 * orbital_count, walkers), jnp.float32),
            pltpu.VMEM((walkers // LANES, electrons * electrons, ROWS, LANES), jnp.float32),
            pltpu.VMEM((electrons * orbital_count * 4, LANES), jnp.float32),
            pltpu.VMEM((GROUP * 2, LANES), jnp.float32),
            pltpu.VMEM((GROUP * 2, LANES), jnp.float32),
        ],
        compiler_params=pltpu.CompilerParams(vmem_limit_bytes=60 * 1024 * 1024),
    )(
        places,
        occupation,
        inverse_slater.reshape(electrons * electrons, walkers),
        orbitals,
        hop_orbitals,
        local_energy[None],
    )
    wide = derivs.astype(jnp.float32)
    sums = jnp.stack(
        [
            jnp.sum(wide, axis=1),
            jnp.sum(wide * wide, axis=1),
            jnp.sum(energy_derivs.astype(jnp.float32), axis=1),
        ]
    )
    return derivs, energy_derivs, sums


def inverse_factor(gram):
    lower_factor = jnp.linalg.cholesky(gram)
    return jax.scipy.linalg.solve_triangular(
        lower_factor, jnp.eye(gram.shape[0], dtype=gram.dtype), lower=True
    )


def on_device(
    occupation, inverse_slater, orbitals, hop_orbitals, local_energy, excitations, initial_block
):
    walker_devices = lax.axis_size("walker")
    local_walkers = local_energy.shape[0]
    walkers = local_walkers * walker_devices
    block_rows = excitations.shape[1]
    count = initial_block.shape[1]
    params = block_rows * lax.axis_size("param")
    owned = block_rows // walker_devices
    derivs, energy_derivs, sums = build(
        occupation, inverse_slater, orbitals, hop_orbitals, local_energy, excitations
    )
    start = initial_block.T

    def across_params(images, grams):
        sent = jnp.concatenate(
            [images.astype(jnp.bfloat16), pad_columns(split_in_three(grams), local_walkers)]
        )
        total = jnp.sum(to_all(sent, "param").astype(jnp.float32), axis=0)
        return total[: 2 * count], joined(total[2 * count :], grams.shape[1])

    images, gram = across_params(
        forward(start, derivs, energy_derivs), dot_nt(start, start)
    )
    factor = inverse_factor(gram)
    totals = jnp.concatenate([dot_nn(factor, images[:count]), dot_nn(factor, images[count:])])
    center = jnp.mean(totals, axis=1)

    offset = lax.axis_index("walker") * owned
    block = dot_nn(factor, lax.dynamic_slice_in_dim(start, offset, owned, 1))
    whole = [dot_nn(factor, start)]
    basis = [block]
    all_totals = [totals]
    all_centers = []
    all_rows = []
    means = s_diagonal = None
    for iteration in range(ITERS + 1):
        row_images = (totals - center[:, None]).astype(jnp.bfloat16)
        wide_rows = row_images.astype(jnp.float32)
        if iteration == ITERS:
            all_centers.append(center)
            all_rows.append(wide_rows)
            break
        back = lax.dot_general(
            row_images, derivs, (((1,), (1,)), ((), ())), preferred_element_type=jnp.float32
        )
        inner = dot_nt(totals[:count], wide_rows)
        if iteration == 0:
            back = back + center[:, None] * sums[0][None]
            inner = inner + local_walkers * center[:count, None] * center[None]
            repeated = jnp.concatenate([inner, local_walkers * center[None]])
            sent = jnp.concatenate([by_owner(back, walker_devices), by_owner(sums, walker_devices)], axis=1)
            repeated = pad_columns(repeated, owned)
        else:
            sent = by_owner(back.astype(jnp.bfloat16), walker_devices)
            repeated = pad_columns(split_in_three(inner), owned)
        sent = jnp.concatenate(
            [sent, jnp.broadcast_to(repeated[None], (walker_devices,) + repeated.shape)], axis=1
        )
        total = jnp.sum(exchange(sent, "walker").astype(jnp.float32), axis=0) / walkers
        if iteration == 0:
            means = jnp.stack([total[2 * count], total[2 * count + 2]])
            s_diagonal = total[2 * count + 1] - means[0] * means[0] + EPS_SHIFT
            inner = total[2 * count + 3 :, : 2 * count]
            common = inner[count]
            wide_rows = wide_rows + (center - common)[:, None]
            center = common
            inner = inner[:count] - center[:count, None] * center[None]
            total = total[: 2 * count] - center[:, None] * means[:1]
        else:
            inner = joined(total[2 * count :], 2 * count)
        all_centers.append(center)
        all_rows.append(wide_rows)
        a_matrix = inner[:, :count] + EPS_SHIFT * jnp.eye(count)
        b_matrix = inner[:, count:] + ENERGY_SHIFT * jnp.eye(count)
        s_image = total[:count] + EPS_SHIFT * block
        h_image = total[count : 2 * count] + ENERGY_SHIFT * block
        rayleigh = jax.scipy.linalg.cho_solve((jnp.linalg.cholesky(a_matrix), True), b_matrix)
        correction = (h_image - dot_nn(rayleigh.T, s_image)) / s_diagonal[None]
        grams = dot_nt(correction, jnp.concatenate(basis + [correction, means]))
        got = to_all(
            jnp.concatenate([correction, pad_columns(grams, 128)], axis=1), "walker"
        )
        grams = jnp.sum(got[:, :, owned : owned + grams.shape[1]], axis=0)
        whole_correction = got[:, :, :owned].transpose(1, 0, 2).reshape(count, block_rows)
        images, grams = across_params(
            forward(whole_correction, derivs, energy_derivs), grams
        )
        earlier = count * (iteration + 1)
        overlap = grams[:, :earlier]
        gram = grams[:, earlier : earlier + count] - dot_nt(overlap, overlap)
        factor = inverse_factor(gram)

        def advance(new, old):
            return dot_nn(factor, new - dot_nn(overlap, old))

        block = advance(correction, jnp.concatenate(basis))
        whole.append(advance(whole_correction, jnp.concatenate(whole)))
        totals = jnp.concatenate(
            [
                advance(images[:count], jnp.concatenate([t[:count] for t in all_totals])),
                advance(images[count:], jnp.concatenate([t[count:] for t in all_totals])),
            ]
        )
        center = jnp.concatenate(
            [
                advance(
                    grams[:, earlier + count + part : earlier + count + part + 1],
                    jnp.concatenate([c[part * count : (part + 1) * count] for c in all_centers])[
                        :, None
                    ],
                )[:, 0]
                for part in range(2)
            ]
        )
        basis.append(block)
        all_totals.append(totals)
    lefts = jnp.concatenate([t[:count] for t in all_totals])
    rights = jnp.concatenate(
        [r[:count] for r in all_rows] + [r[count:] for r in all_rows]
    )
    proj = jnp.sum(to_all(dot_nt(lefts, rights), "walker"), axis=0) / walkers
    size = lefts.shape[0]
    proj_s = proj[:, :size] + EPS_SHIFT * jnp.eye(size)
    proj_h = proj[:, size:] + ENERGY_SHIFT * jnp.eye(size)
    return (math.sqrt(params) * jnp.concatenate(whole).T, proj_h, proj_s)


def solution(mesh):
    placed = (
        P(None, "walker"),
        P(None, None, "walker"),
        P(),
        P(),
        P("walker"),
        P(None, "param"),
        P("param", None),
    )
    return jax.shard_map(
        on_device,
        mesh=mesh,
        in_specs=placed,
        out_specs=(P("param", None), P(), P()),
        check_vma=False,
    )
```

```python
import functools
import math

import jax
import jax.numpy as jnp
from jax import lax
from jax.experimental import pallas as pl
from jax.experimental.pallas import tpu as pltpu
from jax.sharding import PartitionSpec as P

ITERS = 3
EPS_SHIFT = 0.001
ENERGY_SHIFT = 0.5
HIGHEST = lax.Precision.HIGHEST
LANES = 128
ROWS = 8
GROUP = 64


def build_kernel(
    place_ref, occupation_ref, inverse_ref, orbitals_ref, hop_ref, energy_ref,
    derivs_ref, energy_derivs_ref,
    high_ref, low_ref, sites_ref, rows_ref, wide_ref, table_ref, first_ref, second_ref,
):
    electrons, walkers = occupation_ref.shape
    sites, orbitals = orbitals_ref.shape
    params = derivs_ref.shape[0]
    halves = walkers // LANES
    tiles = orbitals // ROWS

    for half in range(halves):
        for row in range(electrons * electrons):
            wide_ref[half, row] = jnp.broadcast_to(
                inverse_ref[row : row + 1, half * LANES : (half + 1) * LANES], (ROWS, LANES)
            )
    for number, source in enumerate((orbitals_ref, hop_ref)):
        for column in range(0, orbitals, LANES):
            turned = source[:, column : column + LANES].T
            high = turned.astype(jnp.bfloat16)
            where = pl.ds(number * orbitals + column, LANES)
            high_ref[where, :] = high
            low_ref[where, :] = (turned - high.astype(jnp.float32)).astype(jnp.bfloat16)

    def pick(electron, carry):
        occupied = occupation_ref[pl.ds(electron, 1), :]
        index = lax.broadcasted_iota(jnp.int32, (sites, walkers), 0)
        sites_ref[...] = jnp.where(index == occupied, 1.0, 0.0).astype(jnp.bfloat16)
        for row in range(0, 2 * orbitals, 256):
            where = pl.ds(row, 256)
            rows_ref[electron, where, :] = jnp.dot(
                high_ref[where, :], sites_ref[...], preferred_element_type=jnp.float32
            ) + jnp.dot(low_ref[where, :], sites_ref[...], preferred_element_type=jnp.float32)
        return carry

    lax.fori_loop(0, electrons, pick, 0)

    def contract(tile, carry):
        for half in range(halves):
            lanes = slice(half * LANES, (half + 1) * LANES)
            plain = [rows_ref[k, pl.ds(pl.multiple_of(tile * ROWS, ROWS), ROWS), lanes] for k in range(electrons)]
            hopped = [
                rows_ref[k, pl.ds(pl.multiple_of(orbitals + tile * ROWS, ROWS), ROWS), lanes]
                for k in range(electrons)
            ]
            scale = energy_ref[0:1, lanes] * 0.5
            for i in range(electrons):
                weight = wide_ref[half, i * electrons]
                ratio = weight * plain[0]
                energy = weight * hopped[0]
                for k in range(1, electrons):
                    weight = wide_ref[half, i * electrons + k]
                    ratio += weight * plain[k]
                    energy += weight * hopped[k]
                base = pl.multiple_of((i * tiles + tile) * 4 * ROWS, ROWS)
                table_ref[pl.ds(base + half, ROWS, stride=4), :] = ratio
                table_ref[pl.ds(base + 2 + half, ROWS, stride=4), :] = energy + scale * ratio
        return carry

    lax.fori_loop(0, tiles, contract, 0)

    def pairs(group, carry):
        for j in range(GROUP):

            def take(which, part):
                return table_ref[pl.ds(pl.multiple_of(place_ref[which * params + group * GROUP + j], 4) + part * 2, 2), :]

            ia, jb, ib, ja = (take(which, 0) for which in range(4))
            e_ia, e_jb, e_ib, e_ja = (take(which, 1) for which in range(4))
            spot = pl.ds(2 * j, 2)
            first_ref[spot, :] = ia * jb - ib * ja
            second_ref[spot, :] = (e_ia * jb + ia * e_jb) - (e_ib * ja + ib * e_ja)
        for source, target in ((first_ref, derivs_ref), (second_ref, energy_derivs_ref)):
            for row in range(0, GROUP, 2 * ROWS):
                for half in range(2):
                    target[
                        pl.ds(pl.multiple_of(group * GROUP + row, 2 * ROWS), 2 * ROWS),
                        half * LANES : (half + 1) * LANES,
                    ] = source[pl.ds(row * 2 + half, 2 * ROWS, stride=2), :].astype(jnp.bfloat16)
        return carry

    lax.fori_loop(0, params // GROUP, pairs, 0)


def build(occupation, inverse_slater, orbitals, hop_orbitals, local_energy, excitations):
    electrons, walkers = occupation.shape
    sites, orbital_count = orbitals.shape
    params = excitations.shape[1]

    def place(electron, orbital):
        row = electron * orbital_count + orbital
        return row * 4

    i, j, a, b = excitations
    places = jnp.concatenate([place(i, a), place(j, b), place(i, b), place(j, a)])
    vmem = pl.BlockSpec(memory_space=pltpu.VMEM)
    derivs, energy_derivs = pl.pallas_call(
        build_kernel,
        out_shape=[jax.ShapeDtypeStruct((params, walkers), jnp.bfloat16)] * 2,
        in_specs=[pl.BlockSpec(memory_space=pltpu.SMEM)] + [vmem] * 5,
        out_specs=[vmem] * 2,
        scratch_shapes=[
            pltpu.VMEM((2 * orbital_count, sites), jnp.bfloat16),
            pltpu.VMEM((2 * orbital_count, sites), jnp.bfloat16),
            pltpu.VMEM((sites, walkers), jnp.bfloat16),
            pltpu.VMEM((electrons, 2 * orbital_count, walkers), jnp.float32),
            pltpu.VMEM((walkers // LANES, electrons * electrons, ROWS, LANES), jnp.float32),
            pltpu.VMEM((electrons * orbital_count * 4, LANES), jnp.float32),
            pltpu.VMEM((GROUP * 2, LANES), jnp.float32),
            pltpu.VMEM((GROUP * 2, LANES), jnp.float32),
        ],
        compiler_params=pltpu.CompilerParams(vmem_limit_bytes=60 * 1024 * 1024),
    )(
        places,
        occupation,
        inverse_slater.reshape(electrons * electrons, walkers),
        orbitals,
        hop_orbitals,
        local_energy[None],
    )
    wide = derivs.astype(jnp.float32)
    sums = jnp.stack(
        [
            jnp.sum(wide, axis=1),
            jnp.sum(wide * wide, axis=1),
            jnp.sum(energy_derivs.astype(jnp.float32), axis=1),
        ]
    )
    return derivs, energy_derivs, sums


def dot_nt(left, right):
    return lax.dot_general(
        left, right, (((1,), (1,)), ((), ())), precision=HIGHEST, preferred_element_type=jnp.float32
    )


def dot_nn(left, right):
    return jnp.dot(left, right, precision=HIGHEST, preferred_element_type=jnp.float32)


def exchange(parts, axis):
    return lax.all_to_all(parts, axis, 0, 0)


def in_thirds(values):
    high = values.astype(jnp.bfloat16).astype(jnp.float32)
    rest = values - high
    middle = rest.astype(jnp.bfloat16).astype(jnp.float32)
    return high, middle, rest - middle


def lanes_of(shape):
    return lax.broadcasted_iota(jnp.int32, shape, 1)


def eliminate(matrix, right, full):
    count = matrix.shape[0]
    row = lax.broadcasted_iota(jnp.int32, (count, 1), 0)
    for j in range(count):
        pivot = matrix[j : j + 1, j : j + 1]
        scale = matrix[:, j : j + 1] / pivot
        keep = (row != j) if full else (row > j)
        scale = jnp.where(keep, scale, 0.0)
        right = right - scale * right[j : j + 1, :]
        matrix = matrix - scale * matrix[j : j + 1, :]
    diagonal = lanes_of(matrix.shape) == lax.broadcasted_iota(jnp.int32, matrix.shape, 0)
    return right, jnp.sum(jnp.where(diagonal, matrix, 0.0), axis=1, keepdims=True)


def advance_kernel(step, share, *refs):
    if step:
        got_ref, own_ref, state_ref, cents_ref, derivs_ref = refs[:5]
        outs = refs[5:]
    else:
        got_ref, own_ref, sums_ref, derivs_ref = refs[:4]
        outs = refs[4:]
    block_ref, tail_ref, grams_ref, rows_ref, sent_ref = outs
    sources, _, width = got_ref.shape
    walkers = width - LANES
    owned = own_ref.shape[1]
    count = own_ref.shape[0]
    total = got_ref[0].astype(jnp.float32)
    for source in range(1, sources):
        total += got_ref[source].astype(jnp.float32)
    part = total[:, walkers:]
    grams = part[:count] + part[count:] + pltpu.roll(part[:count], LANES // 2, 1)
    lane = lanes_of((count, LANES))
    row = lax.broadcasted_iota(jnp.int32, (count, LANES), 0)
    identity = jnp.where(lane == row + LANES // 2, 1.0, 0.0)
    grams = jnp.where(lane < LANES // 2, grams, 0.0)
    grams_ref[...] = grams
    earlier = count * step
    if step:
        tail = jnp.where(lane < 2, pltpu.roll(grams, LANES - (earlier + count), 1), 0.0) + identity
    else:
        tail = identity
    right = jnp.concatenate([own_ref[...], total[:count, :walkers], total[count:, :walkers], tail], axis=1)
    gram = grams
    if step:
        overlap = grams[:, :earlier]
        right = right - dot_nn(overlap, jnp.concatenate([state_ref[...], cents_ref[...]], axis=1))
        gram = pltpu.roll(grams, LANES - earlier, 1)
        padded = jnp.concatenate([overlap, jnp.zeros((LANES - count, earlier), jnp.float32)])
        gram = gram - dot_nt(overlap, padded)
    right, pivots = eliminate(gram, right, False)
    right = right * lax.rsqrt(pivots)
    plain = right[:, owned : owned + walkers]
    energy = right[:, owned + walkers : owned + 2 * walkers]
    block_ref[...] = right[:, : owned + 2 * walkers]
    tail = right[:, owned + 2 * walkers :]
    if step:
        centers = [tail[:, 0:1], tail[:, 1:2]]
    else:
        centers = [jnp.mean(plain, axis=1, keepdims=True), jnp.mean(energy, axis=1, keepdims=True)]
        tail = jnp.where(lane == 0, centers[0], jnp.where(lane == 1, centers[1], tail))
    tail_ref[...] = tail
    center = jnp.concatenate(centers)
    rows = (jnp.concatenate([plain, energy]) - center).astype(jnp.bfloat16)
    wide = rows.astype(jnp.float32)
    rows_ref[...] = wide
    filled = jnp.concatenate([plain, jnp.zeros((LANES - count, walkers), jnp.float32)])
    if step:
        high, middle, low = in_thirds(dot_nt(wide, filled))
        inner = (high + pltpu.roll(middle, 32, 1) + pltpu.roll(low, 64, 1)).astype(jnp.bfloat16)
    else:
        inner = dot_nt(wide + center, filled)
        inner = inner + jnp.where(lanes_of(inner.shape) == count, walkers * center, 0.0)
        across = dot_nt(jnp.ones((count, walkers), jnp.float32), filled)
    for owner in range(sent_ref.shape[0]):
        where = slice(owner * share, (owner + 1) * share)
        back = lax.dot_general(
            rows, derivs_ref[where, :], (((1,), (1,)), ((), ())), preferred_element_type=jnp.float32
        )
        if step:
            sent_ref[owner, :, :share] = back.astype(jnp.bfloat16)
            sent_ref[owner, :, share:] = inner
        else:
            sent_ref[owner, : 2 * count, :share] = back + center * sums_ref[0:1, where]
            sent_ref[owner, : 2 * count, share:] = inner
            sent_ref[owner, 2 * count :, :share] = sums_ref[:, where]
            sent_ref[owner, 2 * count :, share:] = across


def correct_kernel(step, walkers, *refs):
    if step:
        got_ref, state_ref, stats_ref, own_ref, sent_ref, stack_ref = refs
    else:
        got_ref, state_ref, own_ref, sent_ref, stats_ref, cents_ref, stack_ref = refs
    sources, _, width = got_ref.shape
    owned = width - LANES
    count = own_ref.shape[0]
    earlier = count * (step + 1)
    total = got_ref[0].astype(jnp.float32)
    for source in range(1, sources):
        total += got_ref[source].astype(jnp.float32)
    total = total * (1.0 / walkers)
    images = total[: 2 * count, :owned]
    inner = total[: 2 * count, owned:]
    if step:
        inner = inner + pltpu.roll(inner, LANES - 32, 1) + pltpu.roll(inner, LANES - 64, 1)
        stats = stats_ref[...]
    else:
        mean_o = total[2 * count : 2 * count + 1, :owned]
        mean_h = total[2 * count + 2 : 2 * count + 3, :owned]
        square = total[2 * count + 1 : 2 * count + 2, :owned]
        kind = lax.broadcasted_iota(jnp.int32, (count, owned), 0)
        diagonal = square - mean_o * mean_o + EPS_SHIFT
        stats = jnp.where(
            kind == 0, mean_o, jnp.where(kind == 1, mean_h, jnp.where(kind == 2, diagonal, 0.0))
        )
        stats_ref[...] = stats
        center = inner[:, count : count + 1]
        inner = inner - center * total[2 * count : 2 * count + 1, owned:]
        images = images - center * mean_o
        lane = lanes_of((count, LANES))
        cents_ref[...] = jnp.where(
            lane == 0, center[:count], jnp.where(lane == 1, center[count:], 0.0)
        )
    block = state_ref[earlier - count :, :owned]
    lane = lanes_of((count, LANES))
    unit = jnp.where(lane == lax.broadcasted_iota(jnp.int32, lane.shape, 0), 1.0, 0.0)
    a_matrix = jnp.where(lane < count, inner[:count], 0.0) + EPS_SHIFT * unit
    turned_b = inner[count:] + ENERGY_SHIFT * unit
    s_image = images[:count] + EPS_SHIFT * block
    h_image = images[count:] + ENERGY_SHIFT * block
    solved, pivots = eliminate(a_matrix, s_image, True)
    solved = solved / pivots
    correction = h_image - dot_nn(turned_b[:, :count], solved)
    correction = correction / stats[2:3, :]
    own_ref[...] = correction
    stack_ref[...] = jnp.zeros_like(stack_ref)
    stack_ref[:earlier, :] = state_ref[:, :owned]
    stack_ref[earlier : earlier + count, :] = correction
    stack_ref[earlier + count : earlier + 2 * count, :] = stats
    grams = dot_nt(correction, stack_ref[...])
    for target in range(sent_ref.shape[0]):
        sent_ref[target, :, :owned] = correction
        sent_ref[target, :, owned:] = grams


def project_kernel(got_ref, derivs_ref, energy_ref, sent_ref):
    sources, count, width = got_ref.shape
    owned = width - LANES
    grams = jnp.zeros((count, LANES), jnp.float32)
    plain = energy = None
    for source in range(sources):
        values = got_ref[source]
        grams += values[:, owned:]
        values = values[:, :owned]
        high = values.astype(jnp.bfloat16).astype(jnp.float32)
        both = jnp.concatenate([high, values - high]).astype(jnp.bfloat16)
        where = slice(source * owned, (source + 1) * owned)
        more = [
            jnp.dot(both, table[where, :], preferred_element_type=jnp.float32)
            for table in (derivs_ref, energy_ref)
        ]
        plain, energy = more if plain is None else (plain + more[0], energy + more[1])
    images = jnp.concatenate([plain[:count] + plain[count:], energy[:count] + energy[count:]])
    high, middle, low = in_thirds(jnp.where(lanes_of(grams.shape) < LANES // 2, grams, 0.0))
    side = jnp.concatenate([high + pltpu.roll(low, LANES // 2, 1), middle])
    walkers = images.shape[1]
    for target in range(sent_ref.shape[0]):
        sent_ref[target, :, :walkers] = images.astype(jnp.bfloat16)
        sent_ref[target, :, walkers:] = side.astype(jnp.bfloat16)


def stage(body, outs, args, scratch=()):
    vmem = pl.BlockSpec(memory_space=pltpu.VMEM)
    return pl.pallas_call(
        body,
        out_shape=[jax.ShapeDtypeStruct(shape, dtype) for shape, dtype in outs],
        in_specs=[vmem] * len(args),
        out_specs=[vmem] * len(outs),
        scratch_shapes=list(scratch),
        compiler_params=pltpu.CompilerParams(vmem_limit_bytes=20 * 1024 * 1024),
    )(*args)


def on_device(
    occupation, inverse_slater, orbitals, hop_orbitals, local_energy, excitations, initial_block
):
    walker_devices = lax.axis_size("walker")
    param_devices = lax.axis_size("param")
    local_walkers = local_energy.shape[0]
    walkers = local_walkers * walker_devices
    block_rows = excitations.shape[1]
    count = initial_block.shape[1]
    params = block_rows * param_devices
    owned = block_rows // walker_devices
    f32, bf16 = jnp.float32, jnp.bfloat16
    derivs, energy_derivs, sums = build(
        occupation, inverse_slater, orbitals, hop_orbitals, local_energy, excitations
    )
    sums = jnp.pad(sums, ((0, count - sums.shape[0]), (0, 0)))
    start = initial_block.T
    offset = lax.axis_index("walker") * owned
    own = lax.dynamic_slice_in_dim(start, offset, owned, 1)
    gram = jnp.pad(dot_nt(start, start) / walker_devices, ((0, 0), (0, LANES - count)))
    pieces = jnp.concatenate(
        [start.reshape(count, walker_devices, owned).transpose(1, 0, 2),
         jnp.broadcast_to(gram[None], (walker_devices, count, LANES))],
        axis=2,
    )
    state = cents = stats = None
    wholes, plains, rows = [], [], []
    for step in range(ITERS + 1):
        if step:
            pieces = exchange(sent, "walker")
        (sent,) = stage(
            project_kernel,
            [((param_devices, 2 * count, local_walkers + LANES), bf16)],
            (pieces, derivs, energy_derivs),
        )
        got = exchange(sent, "param")
        outs = [
            ((count, owned + 2 * local_walkers), f32),
            ((count, LANES), f32),
            ((count, LANES), f32),
            ((2 * count, local_walkers), f32),
            ((walker_devices, 2 * count, owned + LANES), bf16)
            if step
            else ((walker_devices, 3 * count, owned + LANES), f32),
        ]
        block, tail, grams, wide, sent = stage(
            functools.partial(advance_kernel, step, owned),
            outs,
            (got, own, state, cents, derivs) if step else (got, own, sums, derivs),
        )
        whole = pieces[:, :, :owned].transpose(1, 0, 2).reshape(count, block_rows)
        if step:
            whole = whole - dot_nn(grams[:, : count * step], jnp.concatenate(wholes))
        wholes.append(dot_nn(tail[:, LANES // 2 : LANES // 2 + count], whole))
        plains.append(block[:, owned : owned + local_walkers])
        rows.append(wide)
        state = block if step == 0 else jnp.concatenate([state, block])
        if step == ITERS:
            break
        got = exchange(sent, "walker")
        outs = [
            ((count, owned), f32),
            ((walker_devices, count, owned + LANES), f32),
        ]
        scratch = [pltpu.VMEM((LANES, owned), f32)]
        if step:
            own, sent = stage(
                functools.partial(correct_kernel, step, walkers), outs, (got, state, stats), scratch
            )
            cents = jnp.concatenate(
                [cents, jnp.where(jnp.arange(LANES) < 2, tail, 0.0)]
            )
        else:
            outs += [((count, owned), f32), ((count, LANES), f32)]
            own, sent, stats, cents = stage(
                functools.partial(correct_kernel, step, walkers), outs, (got, state), scratch
            )
            shift = tail[:, :2] - cents[:, :2]
            rows[0] = wide + shift.T.reshape(2 * count, 1)
    lefts = jnp.concatenate(plains)
    rights = jnp.concatenate([r[:count] for r in rows] + [r[count:] for r in rows])
    proj = dot_nt(lefts, rights)
    proj = exchange(jnp.broadcast_to(proj[None], (walker_devices,) + proj.shape), "walker")
    proj = jnp.sum(proj, axis=0) / walkers
    size = lefts.shape[0]
    proj_s = proj[:, :size] + EPS_SHIFT * jnp.eye(size)
    proj_h = proj[:, size:] + ENERGY_SHIFT * jnp.eye(size)
    return (math.sqrt(params) * jnp.concatenate(wholes).T, proj_h, proj_s)


def solution(mesh):
    placed = (
        P(None, "walker"),
        P(None, None, "walker"),
        P(),
        P(),
        P("walker"),
        P(None, "param"),
        P("param", None),
    )
    return jax.shard_map(
        on_device,
        mesh=mesh,
        in_specs=placed,
        out_specs=(P("param", None), P(), P()),
        check_vma=False,
    )
```

```python
import functools
import math

import jax
import jax.numpy as jnp
from jax import lax
from jax.experimental import pallas as pl
from jax.experimental.pallas import tpu as pltpu
from jax.sharding import PartitionSpec as P

ITERS = 3
EPS_SHIFT = 0.001
ENERGY_SHIFT = 0.5
HIGHEST = lax.Precision.HIGHEST
LANES = 128
ROWS = 8
GROUP = 64
COPIES = 4


def build_kernel(
    place_ref, occupation_ref, inverse_ref, orbitals_ref, hop_ref, energy_ref,
    derivs_ref, energy_derivs_ref,
    high_ref, low_ref, sites_ref, rows_ref, wide_ref, table_ref, first_ref, second_ref,
):
    electrons, walkers = occupation_ref.shape
    sites, orbitals = orbitals_ref.shape
    params = derivs_ref.shape[0]
    halves = walkers // LANES
    tiles = orbitals // ROWS

    for half in range(halves):
        for row in range(electrons * electrons):
            wide_ref[half, row] = jnp.broadcast_to(
                inverse_ref[row : row + 1, half * LANES : (half + 1) * LANES], (ROWS, LANES)
            )
    for number, source in enumerate((orbitals_ref, hop_ref)):
        for column in range(0, orbitals, LANES):
            turned = source[:, column : column + LANES].T
            high = turned.astype(jnp.bfloat16)
            where = pl.ds(number * orbitals + column, LANES)
            high_ref[where, :] = high
            low_ref[where, :] = (turned - high.astype(jnp.float32)).astype(jnp.bfloat16)

    def pick(electron, carry):
        occupied = occupation_ref[pl.ds(electron, 1), :]
        index = lax.broadcasted_iota(jnp.int32, (sites, walkers), 0)
        sites_ref[...] = jnp.where(index == occupied, 1.0, 0.0).astype(jnp.bfloat16)
        for row in range(0, 2 * orbitals, 256):
            where = pl.ds(row, 256)
            rows_ref[electron, where, :] = jnp.dot(
                high_ref[where, :], sites_ref[...], preferred_element_type=jnp.float32
            ) + jnp.dot(low_ref[where, :], sites_ref[...], preferred_element_type=jnp.float32)
        return carry

    lax.fori_loop(0, electrons, pick, 0)

    def contract(tile, carry):
        for half in range(halves):
            lanes = slice(half * LANES, (half + 1) * LANES)
            plain = [rows_ref[k, pl.ds(pl.multiple_of(tile * ROWS, ROWS), ROWS), lanes] for k in range(electrons)]
            hopped = [
                rows_ref[k, pl.ds(pl.multiple_of(orbitals + tile * ROWS, ROWS), ROWS), lanes]
                for k in range(electrons)
            ]
            scale = energy_ref[0:1, lanes] * 0.5
            for i in range(electrons):
                weight = wide_ref[half, i * electrons]
                ratio = weight * plain[0]
                energy = weight * hopped[0]
                for k in range(1, electrons):
                    weight = wide_ref[half, i * electrons + k]
                    ratio += weight * plain[k]
                    energy += weight * hopped[k]
                base = pl.multiple_of((i * tiles + tile) * 4 * ROWS, ROWS)
                table_ref[pl.ds(base + half, ROWS, stride=4), :] = ratio
                table_ref[pl.ds(base + 2 + half, ROWS, stride=4), :] = energy + scale * ratio
        return carry

    lax.fori_loop(0, tiles, contract, 0)

    def turned(value):
        return jnp.concatenate([value[2:4], value[0:2]])

    def pairs(group, carry):
        for j in range(GROUP):

            def take(which):
                return table_ref[pl.ds(pl.multiple_of(place_ref[which * params + group * GROUP + j], 4), 4), :]

            ia, jb, ib, ja = (take(which) for which in range(4))
            spot = pl.ds(4 * j, 4)
            first_ref[spot, :] = ia * jb - ib * ja
            second_ref[spot, :] = ia * turned(jb) - ib * turned(ja)
        for source, target, parts in ((first_ref, derivs_ref, 1), (second_ref, energy_derivs_ref, 2)):
            for row in range(0, GROUP, 2 * ROWS):
                for half in range(2):
                    value = source[pl.ds(row * 4 + half, 2 * ROWS, stride=4), :]
                    if parts == 2:
                        value = value + source[pl.ds(row * 4 + 2 + half, 2 * ROWS, stride=4), :]
                    target[
                        pl.ds(pl.multiple_of(group * GROUP + row, 2 * ROWS), 2 * ROWS),
                        half * LANES : (half + 1) * LANES,
                    ] = value.astype(jnp.bfloat16)
        return carry

    lax.fori_loop(0, params // GROUP, pairs, 0)


def build(occupation, inverse_slater, orbitals, hop_orbitals, local_energy, excitations):
    electrons, walkers = occupation.shape
    sites, orbital_count = orbitals.shape
    params = excitations.shape[1]

    def place(electron, orbital):
        row = electron * orbital_count + orbital
        return row * 4

    i, j, a, b = excitations
    places = jnp.concatenate([place(i, a), place(j, b), place(i, b), place(j, a)])
    vmem = pl.BlockSpec(memory_space=pltpu.VMEM)
    derivs, energy_derivs = pl.pallas_call(
        build_kernel,
        out_shape=[jax.ShapeDtypeStruct((params, walkers), jnp.bfloat16)] * 2,
        in_specs=[pl.BlockSpec(memory_space=pltpu.SMEM)] + [vmem] * 5,
        out_specs=[vmem] * 2,
        scratch_shapes=[
            pltpu.VMEM((2 * orbital_count, sites), jnp.bfloat16),
            pltpu.VMEM((2 * orbital_count, sites), jnp.bfloat16),
            pltpu.VMEM((sites, walkers), jnp.bfloat16),
            pltpu.VMEM((electrons, 2 * orbital_count, walkers), jnp.float32),
            pltpu.VMEM((walkers // LANES, electrons * electrons, ROWS, LANES), jnp.float32),
            pltpu.VMEM((electrons * orbital_count * 4, LANES), jnp.float32),
            pltpu.VMEM((GROUP * 4, LANES), jnp.float32),
            pltpu.VMEM((GROUP * 4, LANES), jnp.float32),
        ],
        compiler_params=pltpu.CompilerParams(vmem_limit_bytes=60 * 1024 * 1024),
    )(
        places,
        occupation,
        inverse_slater.reshape(electrons * electrons, walkers),
        orbitals,
        hop_orbitals,
        local_energy[None],
    )
    wide = derivs.astype(jnp.float32)
    sums = jnp.stack(
        [
            jnp.sum(wide, axis=1),
            jnp.sum(wide * wide, axis=1),
            jnp.sum(energy_derivs.astype(jnp.float32), axis=1),
        ]
    )
    return derivs, energy_derivs, sums


def dot_nt(left, right):
    return lax.dot_general(
        left, right, (((1,), (1,)), ((), ())), precision=HIGHEST, preferred_element_type=jnp.float32
    )


def dot_nn(left, right):
    return jnp.dot(left, right, precision=HIGHEST, preferred_element_type=jnp.float32)


def exchange(parts, axis):
    return lax.all_to_all(parts, axis, 0, 0)


def in_thirds(values):
    high = values.astype(jnp.bfloat16).astype(jnp.float32)
    rest = values - high
    middle = rest.astype(jnp.bfloat16).astype(jnp.float32)
    return high, middle, rest - middle


def lanes_of(shape):
    return lax.broadcasted_iota(jnp.int32, shape, 1)


def eliminate(matrix, right, full):
    count = matrix.shape[0]
    row = lax.broadcasted_iota(jnp.int32, (count, 1), 0)
    for j in range(count):
        pivot = matrix[j : j + 1, j : j + 1]
        scale = matrix[:, j : j + 1] / pivot
        keep = (row != j) if full else (row > j)
        scale = jnp.where(keep, scale, 0.0)
        right = right - scale * right[j : j + 1, :]
        matrix = matrix - scale * matrix[j : j + 1, :]
    diagonal = lanes_of(matrix.shape) == lax.broadcasted_iota(jnp.int32, matrix.shape, 0)
    return right, jnp.sum(jnp.where(diagonal, matrix, 0.0), axis=1, keepdims=True)


def advance_kernel(step, share, last, *refs):
    if last:
        got_ref, own_ref, state_ref, cents_ref = refs[:4]
        rows_refs = refs[4 : 4 + step]
        tail_ref, grams_ref, sent_ref = refs[4 + step :]
    elif step:
        got_ref, own_ref, state_ref, cents_ref, derivs_ref = refs[:5]
        block_ref, tail_ref, grams_ref, rows_ref, sent_ref = refs[5:]
    else:
        got_ref, own_ref, sums_ref, derivs_ref = refs[:4]
        block_ref, tail_ref, grams_ref, rows_ref, sent_ref = refs[4:]
    sources, _, width = got_ref.shape
    walkers = width - LANES
    owned = own_ref.shape[1]
    count = own_ref.shape[0]
    total = got_ref[0].astype(jnp.float32)
    for source in range(1, sources):
        total += got_ref[source].astype(jnp.float32)
    part = total[:, walkers:]
    grams = part[:count] + part[count:] + pltpu.roll(part[:count], LANES // 2, 1)
    lane = lanes_of((count, LANES))
    row = lax.broadcasted_iota(jnp.int32, (count, LANES), 0)
    identity = jnp.where(lane == row + LANES // 2, 1.0, 0.0)
    grams = jnp.where(lane < LANES // 2, grams, 0.0)
    grams_ref[...] = grams
    earlier = count * step
    if step:
        tail = jnp.where(lane < 2, pltpu.roll(grams, LANES - (earlier + count), 1), 0.0) + identity
    else:
        tail = identity
    right = jnp.concatenate([own_ref[...], total[:count, :walkers], total[count:, :walkers], tail], axis=1)
    gram = grams
    if step:
        overlap = grams[:, :earlier]
        right = right - dot_nn(overlap, jnp.concatenate([state_ref[...], cents_ref[...]], axis=1))
        gram = pltpu.roll(grams, LANES - earlier, 1)
        padded = jnp.concatenate([overlap, jnp.zeros((LANES - count, earlier), jnp.float32)])
        gram = gram - dot_nt(overlap, padded)
    right, pivots = eliminate(gram, right, False)
    right = right * lax.rsqrt(pivots)
    plain = right[:, owned : owned + walkers]
    energy = right[:, owned + walkers : owned + 2 * walkers]
    if not last:
        block_ref[...] = right[:, : owned + 2 * walkers]
    tail = right[:, owned + 2 * walkers :]
    if step:
        centers = [tail[:, 0:1], tail[:, 1:2]]
    else:
        centers = [jnp.mean(plain, axis=1, keepdims=True), jnp.mean(energy, axis=1, keepdims=True)]
        tail = jnp.where(lane == 0, centers[0], jnp.where(lane == 1, centers[1], tail))
    tail_ref[...] = tail
    center = jnp.concatenate(centers)
    rows = (jnp.concatenate([plain, energy]) - center).astype(jnp.bfloat16)
    wide = rows.astype(jnp.float32)
    if last:
        lefts = jnp.concatenate([state_ref[:, owned : owned + walkers], plain])
        every = [ref[...] for ref in rows_refs] + [wide]
        rights = [value[:count] for value in every] + [value[count:] for value in every]
        size = 2 * count * len(every)
        rights = jnp.concatenate(rights + [jnp.zeros((LANES - size, walkers), jnp.float32)])
        products = dot_nt(lefts, rights)
        for owner in range(sent_ref.shape[0]):
            sent_ref[owner] = products
        return
    rows_ref[...] = wide
    filled = jnp.concatenate([plain, jnp.zeros((LANES - count, walkers), jnp.float32)])
    if step:
        high, middle, low = in_thirds(dot_nt(wide, filled))
        inner = (high + pltpu.roll(middle, 32, 1) + pltpu.roll(low, 64, 1)).astype(jnp.bfloat16)
    else:
        inner = dot_nt(wide + center, filled)
        inner = inner + jnp.where(lanes_of(inner.shape) == count, walkers * center, 0.0)
        across = dot_nt(jnp.ones((count, walkers), jnp.float32), filled)
    for owner in range(sent_ref.shape[0]):
        where = slice(owner * share, (owner + 1) * share)
        back = lax.dot_general(
            rows, derivs_ref[where, :], (((1,), (1,)), ((), ())), preferred_element_type=jnp.float32
        )
        if step:
            sent_ref[owner, :, :share] = back.astype(jnp.bfloat16)
            sent_ref[owner, :, share:] = inner
        else:
            sent_ref[owner, : 2 * count, :share] = back + center * sums_ref[0:1, where]
            sent_ref[owner, : 2 * count, share:] = inner
            sent_ref[owner, 2 * count :, :share] = sums_ref[:, where]
            sent_ref[owner, 2 * count :, share:] = across


def correct_kernel(step, walkers, *refs):
    if step:
        got_ref, state_ref, stats_ref, own_ref, sent_ref, stack_ref = refs
    else:
        got_ref, state_ref, own_ref, sent_ref, stats_ref, cents_ref, stack_ref = refs
    sources, _, width = got_ref.shape
    owned = width - LANES
    count = own_ref.shape[0]
    earlier = count * (step + 1)
    total = got_ref[0].astype(jnp.float32)
    for source in range(1, sources):
        total += got_ref[source].astype(jnp.float32)
    total = total * (1.0 / walkers)
    images = total[: 2 * count, :owned]
    inner = total[: 2 * count, owned:]
    if step:
        inner = inner + pltpu.roll(inner, LANES - 32, 1) + pltpu.roll(inner, LANES - 64, 1)
        stats = stats_ref[...]
    else:
        mean_o = total[2 * count : 2 * count + 1, :owned]
        mean_h = total[2 * count + 2 : 2 * count + 3, :owned]
        square = total[2 * count + 1 : 2 * count + 2, :owned]
        kind = lax.broadcasted_iota(jnp.int32, (count, owned), 0)
        diagonal = square - mean_o * mean_o + EPS_SHIFT
        stats = jnp.where(
            kind == 0, mean_o, jnp.where(kind == 1, mean_h, jnp.where(kind == 2, diagonal, 0.0))
        )
        stats_ref[...] = stats
        center = inner[:, count : count + 1]
        inner = inner - center * total[2 * count : 2 * count + 1, owned:]
        images = images - center * mean_o
        lane = lanes_of((count, LANES))
        cents_ref[...] = jnp.where(
            lane == 0, center[:count], jnp.where(lane == 1, center[count:], 0.0)
        )
    block = state_ref[earlier - count :, :owned]
    lane = lanes_of((count, LANES))
    unit = jnp.where(lane == lax.broadcasted_iota(jnp.int32, lane.shape, 0), 1.0, 0.0)
    a_matrix = jnp.where(lane < count, inner[:count], 0.0) + EPS_SHIFT * unit
    turned_b = inner[count:] + ENERGY_SHIFT * unit
    s_image = images[:count] + EPS_SHIFT * block
    h_image = images[count:] + ENERGY_SHIFT * block
    solved, pivots = eliminate(a_matrix, s_image, True)
    solved = solved / pivots
    correction = h_image - dot_nn(turned_b[:, :count], solved)
    correction = correction / stats[2:3, :]
    own_ref[...] = correction
    stack_ref[...] = jnp.zeros_like(stack_ref)
    stack_ref[:earlier, :] = state_ref[:, :owned]
    stack_ref[earlier : earlier + count, :] = correction
    stack_ref[earlier + count : earlier + 2 * count, :] = stats
    grams = dot_nt(correction, stack_ref[...])
    for target in range(sent_ref.shape[0]):
        sent_ref[target, :, :owned] = correction
        sent_ref[target, :, owned:] = grams


def project_kernel(got_ref, derivs_ref, energy_ref, sent_ref, plain_ref, wide_ref, sems):
    sources, count, width = got_ref.shape
    owned = width - LANES
    rows = plain_ref.shape[0]
    chunk = rows // COPIES
    copies = []
    for part in range(COPIES):
        where = pl.ds(part * chunk, chunk)
        for number, (source, target) in enumerate(((derivs_ref, plain_ref), (energy_ref, wide_ref))):
            copies.append(
                pltpu.make_async_copy(source.at[where, :], target.at[where, :], sems.at[part, number])
            )
            copies[-1].start()
    grams = jnp.zeros((count, LANES), jnp.float32)
    for source in range(sources):
        grams += got_ref[source, :, owned:]
    high, middle, low = in_thirds(jnp.where(lanes_of(grams.shape) < LANES // 2, grams, 0.0))
    side = jnp.concatenate([high + pltpu.roll(low, LANES // 2, 1), middle]).astype(jnp.bfloat16)
    plain = energy = None
    for part in range(COPIES):
        copies[2 * part].wait()
        copies[2 * part + 1].wait()
        for source in range(part * sources // COPIES, (part + 1) * sources // COPIES):
            values = got_ref[source, :, :owned]
            high = values.astype(jnp.bfloat16).astype(jnp.float32)
            both = jnp.concatenate([high, values - high]).astype(jnp.bfloat16)
            where = slice(source * owned, (source + 1) * owned)
            more = [
                jnp.dot(both, table[where, :], preferred_element_type=jnp.float32)
                for table in (plain_ref, wide_ref)
            ]
            plain, energy = more if plain is None else (plain + more[0], energy + more[1])
    images = jnp.concatenate([plain[:count] + plain[count:], energy[:count] + energy[count:]])
    images = images.astype(jnp.bfloat16)
    walkers = images.shape[1]
    for target in range(sent_ref.shape[0]):
        sent_ref[target, :, :walkers] = images
        sent_ref[target, :, walkers:] = side


def finish_kernel(walkers, got_ref, first_ref, second_ref):
    total = got_ref[0]
    for source in range(1, got_ref.shape[0]):
        total += got_ref[source]
    total = total * (1.0 / walkers)
    size = first_ref.shape[0]
    unit = jnp.where(lanes_of(total.shape) == lax.broadcasted_iota(jnp.int32, total.shape, 0), 1.0, 0.0)
    first_ref[...] = (pltpu.roll(total, LANES - size, 1) + ENERGY_SHIFT * unit)[:, :size]
    second_ref[...] = (total + EPS_SHIFT * unit)[:, :size]


def stage(body, outs, args, scratch=(), outside=0, limit=20):
    vmem = pl.BlockSpec(memory_space=pltpu.VMEM)
    return pl.pallas_call(
        body,
        out_shape=[jax.ShapeDtypeStruct(shape, dtype) for shape, dtype in outs],
        in_specs=[vmem] * (len(args) - outside) + [pl.BlockSpec(memory_space=pl.ANY)] * outside,
        out_specs=[vmem] * len(outs),
        scratch_shapes=list(scratch),
        compiler_params=pltpu.CompilerParams(vmem_limit_bytes=limit * 1024 * 1024),
    )(*args)


def on_device(
    occupation, inverse_slater, orbitals, hop_orbitals, local_energy, excitations, initial_block
):
    walker_devices = lax.axis_size("walker")
    param_devices = lax.axis_size("param")
    local_walkers = local_energy.shape[0]
    walkers = local_walkers * walker_devices
    block_rows = excitations.shape[1]
    count = initial_block.shape[1]
    params = block_rows * param_devices
    owned = block_rows // walker_devices
    f32, bf16 = jnp.float32, jnp.bfloat16
    derivs, energy_derivs, sums = build(
        occupation, inverse_slater, orbitals, hop_orbitals, local_energy, excitations
    )
    sums = jnp.pad(sums, ((0, count - sums.shape[0]), (0, 0)))
    start = initial_block.T
    offset = lax.axis_index("walker") * owned
    own = lax.dynamic_slice_in_dim(start, offset, owned, 1)
    gram = jnp.pad(dot_nt(start, start) / walker_devices, ((0, 0), (0, LANES - count)))
    pieces = jnp.concatenate(
        [start.reshape(count, walker_devices, owned).transpose(1, 0, 2),
         jnp.broadcast_to(gram[None], (walker_devices, count, LANES))],
        axis=2,
    )
    state = cents = stats = None
    wholes, rows = [], []
    for step in range(ITERS + 1):
        if step:
            pieces = exchange(sent, "walker")
        (sent,) = stage(
            project_kernel,
            [((param_devices, 2 * count, local_walkers + LANES), bf16)],
            (pieces, derivs, energy_derivs),
            [pltpu.VMEM(derivs.shape, bf16)] * 2 + [pltpu.SemaphoreType.DMA((COPIES, 2))],
            2,
            60,
        )
        got = exchange(sent, "param")
        last = step == ITERS
        body = functools.partial(advance_kernel, step, owned, last)
        if last:
            tail, grams, sent = stage(
                body,
                [
                    ((count, LANES), f32),
                    ((count, LANES), f32),
                    ((walker_devices, count * (ITERS + 1), LANES), f32),
                ],
                (got, own, state, cents, *rows),
            )
        else:
            outs = [
                ((count, owned + 2 * local_walkers), f32),
                ((count, LANES), f32),
                ((count, LANES), f32),
                ((2 * count, local_walkers), f32),
                ((walker_devices, 2 * count, owned + LANES), bf16)
                if step
                else ((walker_devices, 3 * count, owned + LANES), f32),
            ]
            block, tail, grams, wide, sent = stage(
                body, outs, (got, own, state, cents, derivs) if step else (got, own, sums, derivs)
            )
        whole = pieces[:, :, :owned].transpose(1, 0, 2).reshape(count, block_rows)
        if step:
            whole = whole - dot_nn(grams[:, : count * step], jnp.concatenate(wholes))
        wholes.append(dot_nn(tail[:, LANES // 2 : LANES // 2 + count], whole))
        if last:
            break
        rows.append(wide)
        state = block if step == 0 else jnp.concatenate([state, block])
        got = exchange(sent, "walker")
        outs = [
            ((count, owned), f32),
            ((walker_devices, count, owned + LANES), f32),
        ]
        scratch = [pltpu.VMEM((LANES, owned), f32)]
        if step:
            own, sent = stage(
                functools.partial(correct_kernel, step, walkers), outs, (got, state, stats), scratch
            )
            cents = jnp.concatenate(
                [cents, jnp.where(jnp.arange(LANES) < 2, tail, 0.0)]
            )
        else:
            outs += [((count, owned), f32), ((count, LANES), f32)]
            own, sent, stats, cents = stage(
                functools.partial(correct_kernel, step, walkers), outs, (got, state), scratch
            )
            shift = tail[:, :2] - cents[:, :2]
            rows[0] = wide + shift.T.reshape(2 * count, 1)
    size = count * (ITERS + 1)
    proj_h, proj_s = stage(
        functools.partial(finish_kernel, walkers),
        [((size, size), f32)] * 2,
        (exchange(sent, "walker"),),
    )
    return (math.sqrt(params) * jnp.concatenate(wholes).T, proj_h, proj_s)


def solution(mesh):
    placed = (
        P(None, "walker"),
        P(None, None, "walker"),
        P(),
        P(),
        P("walker"),
        P(None, "param"),
        P("param", None),
    )
    return jax.shard_map(
        on_device,
        mesh=mesh,
        in_specs=placed,
        out_specs=(P("param", None), P(), P()),
        check_vma=False,
    )
```

```python
import functools
import math

import jax
import jax.numpy as jnp
from jax import lax
from jax.experimental import pallas as pl
from jax.experimental.pallas import tpu as pltpu
from jax.sharding import PartitionSpec as P

ITERS = 3
EPS_SHIFT = 0.001
ENERGY_SHIFT = 0.5
HIGHEST = lax.Precision.HIGHEST
LANES = 128
ROWS = 8
GROUP = 64


def build_kernel(
    place_ref, occupation_ref, inverse_ref, orbitals_ref, hop_ref, energy_ref,
    derivs_ref, energy_derivs_ref,
    high_ref, low_ref, sites_ref, rows_ref, wide_ref, table_ref, first_ref, second_ref,
):
    electrons, walkers = occupation_ref.shape
    sites, orbitals = orbitals_ref.shape
    params = derivs_ref.shape[0]
    halves = walkers // LANES
    tiles = orbitals // ROWS

    for half in range(halves):
        for row in range(electrons * electrons):
            wide_ref[half, row] = jnp.broadcast_to(
                inverse_ref[row : row + 1, half * LANES : (half + 1) * LANES], (ROWS, LANES)
            )
    for number, source in enumerate((orbitals_ref, hop_ref)):
        for column in range(0, orbitals, LANES):
            turned = source[:, column : column + LANES].T
            high = turned.astype(jnp.bfloat16)
            where = pl.ds(number * orbitals + column, LANES)
            high_ref[where, :] = high
            low_ref[where, :] = (turned - high.astype(jnp.float32)).astype(jnp.bfloat16)

    def pick(electron, carry):
        occupied = occupation_ref[pl.ds(electron, 1), :]
        index = lax.broadcasted_iota(jnp.int32, (sites, walkers), 0)
        sites_ref[...] = jnp.where(index == occupied, 1.0, 0.0).astype(jnp.bfloat16)
        for row in range(0, 2 * orbitals, 256):
            where = pl.ds(row, 256)
            rows_ref[electron, where, :] = jnp.dot(
                high_ref[where, :], sites_ref[...], preferred_element_type=jnp.float32
            ) + jnp.dot(low_ref[where, :], sites_ref[...], preferred_element_type=jnp.float32)
        return carry

    lax.fori_loop(0, electrons, pick, 0)

    def contract(tile, carry):
        for half in range(halves):
            lanes = slice(half * LANES, (half + 1) * LANES)
            plain = [rows_ref[k, pl.ds(pl.multiple_of(tile * ROWS, ROWS), ROWS), lanes] for k in range(electrons)]
            hopped = [
                rows_ref[k, pl.ds(pl.multiple_of(orbitals + tile * ROWS, ROWS), ROWS), lanes]
                for k in range(electrons)
            ]
            scale = energy_ref[0:1, lanes] * 0.5
            for i in range(electrons):
                weight = wide_ref[half, i * electrons]
                ratio = weight * plain[0]
                energy = weight * hopped[0]
                for k in range(1, electrons):
                    weight = wide_ref[half, i * electrons + k]
                    ratio += weight * plain[k]
                    energy += weight * hopped[k]
                base = pl.multiple_of((i * tiles + tile) * 4 * ROWS, ROWS)
                table_ref[pl.ds(base + half, ROWS, stride=4), :] = ratio
                table_ref[pl.ds(base + 2 + half, ROWS, stride=4), :] = energy + scale * ratio
        return carry

    lax.fori_loop(0, tiles, contract, 0)

    def turned(value):
        return jnp.concatenate([value[2:4], value[0:2]])

    def pairs(group, carry):
        for j in range(GROUP):

            def take(which):
                return table_ref[pl.ds(pl.multiple_of(place_ref[which * params + group * GROUP + j], 4), 4), :]

            ia, jb, ib, ja = (take(which) for which in range(4))
            spot = pl.ds(4 * j, 4)
            first_ref[spot, :] = ia * jb - ib * ja
            second_ref[spot, :] = ia * turned(jb) - ib * turned(ja)
        for source, target, parts in ((first_ref, derivs_ref, 1), (second_ref, energy_derivs_ref, 2)):
            for row in range(0, GROUP, 2 * ROWS):
                for half in range(2):
                    value = source[pl.ds(row * 4 + half, 2 * ROWS, stride=4), :]
                    if parts == 2:
                        value = value + source[pl.ds(row * 4 + 2 + half, 2 * ROWS, stride=4), :]
                    target[
                        pl.ds(pl.multiple_of(group * GROUP + row, 2 * ROWS), 2 * ROWS),
                        half * LANES : (half + 1) * LANES,
                    ] = value.astype(jnp.bfloat16)
        return carry

    lax.fori_loop(0, params // GROUP, pairs, 0)


def build(occupation, inverse_slater, orbitals, hop_orbitals, local_energy, excitations):
    electrons, walkers = occupation.shape
    sites, orbital_count = orbitals.shape
    params = excitations.shape[1]

    def place(electron, orbital):
        row = electron * orbital_count + orbital
        return row * 4

    i, j, a, b = excitations
    places = jnp.concatenate([place(i, a), place(j, b), place(i, b), place(j, a)])
    vmem = pl.BlockSpec(memory_space=pltpu.VMEM)
    return pl.pallas_call(
        build_kernel,
        out_shape=[jax.ShapeDtypeStruct((params, walkers), jnp.bfloat16)] * 2,
        in_specs=[pl.BlockSpec(memory_space=pltpu.SMEM)] + [vmem] * 5,
        out_specs=[vmem] * 2,
        scratch_shapes=[
            pltpu.VMEM((2 * orbital_count, sites), jnp.bfloat16),
            pltpu.VMEM((2 * orbital_count, sites), jnp.bfloat16),
            pltpu.VMEM((sites, walkers), jnp.bfloat16),
            pltpu.VMEM((electrons, 2 * orbital_count, walkers), jnp.float32),
            pltpu.VMEM((walkers // LANES, electrons * electrons, ROWS, LANES), jnp.float32),
            pltpu.VMEM((electrons * orbital_count * 4, LANES), jnp.float32),
            pltpu.VMEM((GROUP * 4, LANES), jnp.float32),
            pltpu.VMEM((GROUP * 4, LANES), jnp.float32),
        ],
        compiler_params=pltpu.CompilerParams(vmem_limit_bytes=49 * 1024 * 1024),
    )(
        places,
        occupation,
        inverse_slater.reshape(electrons * electrons, walkers),
        orbitals,
        hop_orbitals,
        local_energy[None],
    )

def walker_sums(derivs, energy_derivs):
    wide = derivs.astype(jnp.float32)
    return jnp.stack(
        [
            jnp.sum(wide, axis=1),
            jnp.sum(wide * wide, axis=1),
            jnp.sum(energy_derivs.astype(jnp.float32), axis=1),
        ]
    )


def dot_nt(left, right):
    return lax.dot_general(
        left, right, (((1,), (1,)), ((), ())), precision=HIGHEST, preferred_element_type=jnp.float32
    )


def dot_nn(left, right):
    return jnp.dot(left, right, precision=HIGHEST, preferred_element_type=jnp.float32)


def exchange(parts, axis):
    return lax.all_to_all(parts, axis, 0, 0)


def in_thirds(values):
    high = values.astype(jnp.bfloat16).astype(jnp.float32)
    rest = values - high
    middle = rest.astype(jnp.bfloat16).astype(jnp.float32)
    return high, middle, rest - middle


def lanes_of(shape):
    return lax.broadcasted_iota(jnp.int32, shape, 1)


def eliminate(matrix, right, full):
    count = matrix.shape[0]
    row = lax.broadcasted_iota(jnp.int32, (count, 1), 0)
    for j in range(count):
        pivot = matrix[j : j + 1, j : j + 1]
        scale = matrix[:, j : j + 1] / pivot
        keep = (row != j) if full else (row > j)
        scale = jnp.where(keep, scale, 0.0)
        right = right - scale * right[j : j + 1, :]
        matrix = matrix - scale * matrix[j : j + 1, :]
    diagonal = lanes_of(matrix.shape) == lax.broadcasted_iota(jnp.int32, matrix.shape, 0)
    return right, jnp.sum(jnp.where(diagonal, matrix, 0.0), axis=1, keepdims=True)


def advance_kernel(step, share, last, *refs):
    if last:
        got_ref, own_ref, state_ref, cents_ref = refs[:4]
        rows_refs = refs[4 : 4 + step]
        tail_ref, grams_ref, sent_ref = refs[4 + step :]
    elif step:
        got_ref, own_ref, state_ref, cents_ref, derivs_ref = refs[:5]
        block_ref, tail_ref, grams_ref, rows_ref, sent_ref = refs[5:]
    else:
        got_ref, own_ref, sums_ref, derivs_ref = refs[:4]
        block_ref, tail_ref, grams_ref, rows_ref, sent_ref = refs[4:]
    sources, _, width = got_ref.shape
    walkers = width - LANES
    owned = own_ref.shape[1]
    count = own_ref.shape[0]
    total = got_ref[0].astype(jnp.float32)
    for source in range(1, sources):
        total += got_ref[source].astype(jnp.float32)
    part = total[:, walkers:]
    grams = part[:count] + part[count:] + pltpu.roll(part[:count], LANES // 2, 1)
    lane = lanes_of((count, LANES))
    row = lax.broadcasted_iota(jnp.int32, (count, LANES), 0)
    identity = jnp.where(lane == row + LANES // 2, 1.0, 0.0)
    grams = jnp.where(lane < LANES // 2, grams, 0.0)
    grams_ref[...] = grams
    earlier = count * step
    if step:
        tail = jnp.where(lane < 2, pltpu.roll(grams, LANES - (earlier + count), 1), 0.0) + identity
    else:
        tail = identity
    right = jnp.concatenate([own_ref[...], total[:count, :walkers], total[count:, :walkers], tail], axis=1)
    gram = grams
    if step:
        overlap = grams[:, :earlier]
        right = right - dot_nn(overlap, jnp.concatenate([state_ref[...], cents_ref[...]], axis=1))
        gram = pltpu.roll(grams, LANES - earlier, 1)
        padded = jnp.concatenate([overlap, jnp.zeros((LANES - count, earlier), jnp.float32)])
        gram = gram - dot_nt(overlap, padded)
    right, pivots = eliminate(gram, right, False)
    right = right * lax.rsqrt(pivots)
    plain = right[:, owned : owned + walkers]
    energy = right[:, owned + walkers : owned + 2 * walkers]
    if not last:
        block_ref[...] = right[:, : owned + 2 * walkers]
    tail = right[:, owned + 2 * walkers :]
    if step:
        centers = [tail[:, 0:1], tail[:, 1:2]]
    else:
        centers = [jnp.mean(plain, axis=1, keepdims=True), jnp.mean(energy, axis=1, keepdims=True)]
        tail = jnp.where(lane == 0, centers[0], jnp.where(lane == 1, centers[1], tail))
    tail_ref[...] = tail
    center = jnp.concatenate(centers)
    rows = (jnp.concatenate([plain, energy]) - center).astype(jnp.bfloat16)
    wide = rows.astype(jnp.float32)
    if last:
        lefts = jnp.concatenate([state_ref[:, owned : owned + walkers], plain])
        every = [ref[...] for ref in rows_refs] + [wide]
        rights = [value[:count] for value in every] + [value[count:] for value in every]
        size = 2 * count * len(every)
        rights = jnp.concatenate(rights + [jnp.zeros((LANES - size, walkers), jnp.float32)])
        products = dot_nt(lefts, rights)
        for owner in range(sent_ref.shape[0]):
            sent_ref[owner] = products
        return
    rows_ref[...] = wide
    filled = jnp.concatenate([plain, jnp.zeros((LANES - count, walkers), jnp.float32)])
    if step:
        high, middle, low = in_thirds(dot_nt(wide, filled))
        inner = (high + pltpu.roll(middle, 32, 1) + pltpu.roll(low, 64, 1)).astype(jnp.bfloat16)
    else:
        inner = dot_nt(wide + center, filled)
        inner = inner + jnp.where(lanes_of(inner.shape) == count, walkers * center, 0.0)
        across = dot_nt(jnp.ones((count, walkers), jnp.float32), filled)
    for owner in range(sent_ref.shape[0]):
        where = slice(owner * share, (owner + 1) * share)
        back = lax.dot_general(
            rows, derivs_ref[where, :], (((1,), (1,)), ((), ())), preferred_element_type=jnp.float32
        )
        if step:
            sent_ref[owner, :, :share] = back.astype(jnp.bfloat16)
            sent_ref[owner, :, share:] = inner
        else:
            sent_ref[owner, : 2 * count, :share] = back + center * sums_ref[0:1, where]
            sent_ref[owner, : 2 * count, share:] = inner
            sent_ref[owner, 2 * count :, :share] = sums_ref[:, where]
            sent_ref[owner, 2 * count :, share:] = across


def correct_kernel(step, walkers, *refs):
    if step:
        got_ref, state_ref, stats_ref, own_ref, sent_ref, stack_ref = refs
    else:
        got_ref, state_ref, own_ref, sent_ref, stats_ref, cents_ref, stack_ref = refs
    sources, _, width = got_ref.shape
    owned = width - LANES
    count = own_ref.shape[0]
    earlier = count * (step + 1)
    total = got_ref[0].astype(jnp.float32)
    for source in range(1, sources):
        total += got_ref[source].astype(jnp.float32)
    total = total * (1.0 / walkers)
    images = total[: 2 * count, :owned]
    inner = total[: 2 * count, owned:]
    if step:
        inner = inner + pltpu.roll(inner, LANES - 32, 1) + pltpu.roll(inner, LANES - 64, 1)
        stats = stats_ref[...]
    else:
        mean_o = total[2 * count : 2 * count + 1, :owned]
        mean_h = total[2 * count + 2 : 2 * count + 3, :owned]
        square = total[2 * count + 1 : 2 * count + 2, :owned]
        kind = lax.broadcasted_iota(jnp.int32, (count, owned), 0)
        diagonal = square - mean_o * mean_o + EPS_SHIFT
        stats = jnp.where(
            kind == 0, mean_o, jnp.where(kind == 1, mean_h, jnp.where(kind == 2, diagonal, 0.0))
        )
        stats_ref[...] = stats
        center = inner[:, count : count + 1]
        inner = inner - center * total[2 * count : 2 * count + 1, owned:]
        images = images - center * mean_o
        lane = lanes_of((count, LANES))
        cents_ref[...] = jnp.where(
            lane == 0, center[:count], jnp.where(lane == 1, center[count:], 0.0)
        )
    block = state_ref[earlier - count :, :owned]
    lane = lanes_of((count, LANES))
    unit = jnp.where(lane == lax.broadcasted_iota(jnp.int32, lane.shape, 0), 1.0, 0.0)
    a_matrix = jnp.where(lane < count, inner[:count], 0.0) + EPS_SHIFT * unit
    turned_b = inner[count:] + ENERGY_SHIFT * unit
    s_image = images[:count] + EPS_SHIFT * block
    h_image = images[count:] + ENERGY_SHIFT * block
    solved, pivots = eliminate(a_matrix, s_image, True)
    solved = solved / pivots
    correction = h_image - dot_nn(turned_b[:, :count], solved)
    correction = correction / stats[2:3, :]
    own_ref[...] = correction
    stack_ref[...] = jnp.zeros_like(stack_ref)
    stack_ref[:earlier, :] = state_ref[:, :owned]
    stack_ref[earlier : earlier + count, :] = correction
    stack_ref[earlier + count : earlier + 2 * count, :] = stats
    grams = dot_nt(correction, stack_ref[...])
    for target in range(sent_ref.shape[0]):
        sent_ref[target, :, :owned] = correction
        sent_ref[target, :, owned:] = grams


def project_kernel(first, got_ref, derivs_ref, energy_ref, sent_ref):
    params = derivs_ref.shape[0]
    if first:
        count, sources, owned = got_ref.shape[0], 1, params
    else:
        sources, count, width = got_ref.shape
        owned = width - LANES
    grams = jnp.zeros((count, LANES), jnp.float32)
    plain = energy = None
    for source in range(sources):
        if first:
            values = got_ref[...]
            grams = jnp.concatenate(
                [dot_nt(values, values), jnp.zeros((count, LANES - count), jnp.float32)], axis=1
            )
        else:
            values = got_ref[source, :, :owned]
            grams += got_ref[source, :, owned:]
        high = values.astype(jnp.bfloat16).astype(jnp.float32)
        both = jnp.concatenate([high, values - high]).astype(jnp.bfloat16)
        more = [
            jnp.dot(
                both,
                table[source * owned : (source + 1) * owned, :],
                preferred_element_type=jnp.float32,
            )
            for table in (derivs_ref, energy_ref)
        ]
        plain, energy = more if plain is None else (plain + more[0], energy + more[1])
    images = jnp.concatenate([plain[:count] + plain[count:], energy[:count] + energy[count:]])
    images = images.astype(jnp.bfloat16)
    high, middle, low = in_thirds(jnp.where(lanes_of(grams.shape) < LANES // 2, grams, 0.0))
    side = jnp.concatenate([high + pltpu.roll(low, LANES // 2, 1), middle]).astype(jnp.bfloat16)
    walkers = images.shape[1]
    for target in range(sent_ref.shape[0]):
        sent_ref[target, :, :walkers] = images
        sent_ref[target, :, walkers:] = side


def finish_kernel(walkers, got_ref, first_ref, second_ref):
    total = got_ref[0]
    for source in range(1, got_ref.shape[0]):
        total += got_ref[source]
    total = total * (1.0 / walkers)
    size = first_ref.shape[0]
    unit = jnp.where(lanes_of(total.shape) == lax.broadcasted_iota(jnp.int32, total.shape, 0), 1.0, 0.0)
    first_ref[...] = (pltpu.roll(total, LANES - size, 1) + ENERGY_SHIFT * unit)[:, :size]
    second_ref[...] = (total + EPS_SHIFT * unit)[:, :size]


def stage(body, outs, args, scratch=()):
    vmem = pl.BlockSpec(memory_space=pltpu.VMEM)
    return pl.pallas_call(
        body,
        out_shape=[jax.ShapeDtypeStruct(shape, dtype) for shape, dtype in outs],
        in_specs=[vmem] * len(args),
        out_specs=[vmem] * len(outs),
        scratch_shapes=list(scratch),
        compiler_params=pltpu.CompilerParams(vmem_limit_bytes=20 * 1024 * 1024),
    )(*args)


def on_device(
    occupation, inverse_slater, orbitals, hop_orbitals, local_energy, excitations, initial_block
):
    walker_devices = lax.axis_size("walker")
    param_devices = lax.axis_size("param")
    local_walkers = local_energy.shape[0]
    walkers = local_walkers * walker_devices
    block_rows = excitations.shape[1]
    count = initial_block.shape[1]
    params = block_rows * param_devices
    owned = block_rows // walker_devices
    f32, bf16 = jnp.float32, jnp.bfloat16
    derivs, energy_derivs = build(
        occupation, inverse_slater, orbitals, hop_orbitals, local_energy, excitations
    )
    sums = walker_sums(derivs, energy_derivs)
    sums = jnp.pad(sums, ((0, count - sums.shape[0]), (0, 0)))
    start = initial_block.T
    offset = lax.axis_index("walker") * owned
    own = lax.dynamic_slice_in_dim(start, offset, owned, 1)
    state = cents = stats = None
    wholes, rows = [], []
    for step in range(ITERS + 1):
        if step:
            pieces = exchange(sent, "walker")
        (sent,) = stage(
            functools.partial(project_kernel, step == 0),
            [((param_devices, 2 * count, local_walkers + LANES), bf16)],
            (pieces if step else start, derivs, energy_derivs),
        )
        got = exchange(sent, "param")
        last = step == ITERS
        body = functools.partial(advance_kernel, step, owned, last)
        if last:
            tail, grams, sent = stage(
                body,
                [
                    ((count, LANES), f32),
                    ((count, LANES), f32),
                    ((walker_devices, count * (ITERS + 1), LANES), f32),
                ],
                (got, own, state, cents, *rows),
            )
        else:
            outs = [
                ((count, owned + 2 * local_walkers), f32),
                ((count, LANES), f32),
                ((count, LANES), f32),
                ((2 * count, local_walkers), f32),
                ((walker_devices, 2 * count, owned + LANES), bf16)
                if step
                else ((walker_devices, 3 * count, owned + LANES), f32),
            ]
            block, tail, grams, wide, sent = stage(
                body, outs, (got, own, state, cents, derivs) if step else (got, own, sums, derivs)
            )
        whole = start
        if step:
            whole = pieces[:, :, :owned].transpose(1, 0, 2).reshape(count, block_rows)
            whole = whole - dot_nn(grams[:, : count * step], jnp.concatenate(wholes))
        wholes.append(dot_nn(tail[:, LANES // 2 : LANES // 2 + count], whole))
        if last:
            break
        rows.append(wide)
        state = block if step == 0 else jnp.concatenate([state, block])
        got = exchange(sent, "walker")
        outs = [
            ((count, owned), f32),
            ((walker_devices, count, owned + LANES), f32),
        ]
        scratch = [pltpu.VMEM((LANES, owned), f32)]
        if step:
            own, sent = stage(
                functools.partial(correct_kernel, step, walkers), outs, (got, state, stats), scratch
            )
            cents = jnp.concatenate(
                [cents, jnp.where(jnp.arange(LANES) < 2, tail, 0.0)]
            )
        else:
            outs += [((count, owned), f32), ((count, LANES), f32)]
            own, sent, stats, cents = stage(
                functools.partial(correct_kernel, step, walkers), outs, (got, state), scratch
            )
            shift = tail[:, :2] - cents[:, :2]
            rows[0] = wide + shift.T.reshape(2 * count, 1)
    size = count * (ITERS + 1)
    proj_h, proj_s = stage(
        functools.partial(finish_kernel, walkers),
        [((size, size), f32)] * 2,
        (exchange(sent, "walker"),),
    )
    return (math.sqrt(params) * jnp.concatenate(wholes).T, proj_h, proj_s)


def solution(mesh):
    placed = (
        P(None, "walker"),
        P(None, None, "walker"),
        P(),
        P(),
        P("walker"),
        P(None, "param"),
        P("param", None),
    )
    return jax.shard_map(
        on_device,
        mesh=mesh,
        in_specs=placed,
        out_specs=(P("param", None), P(), P()),
        check_vma=False,
    )
```

```python
import functools
import math

import jax
import jax.numpy as jnp
from jax import lax
from jax.experimental import pallas as pl
from jax.experimental.pallas import tpu as pltpu
from jax.sharding import PartitionSpec as P

ITERS = 3
EPS_SHIFT = 0.001
ENERGY_SHIFT = 0.5
HIGHEST = lax.Precision.HIGHEST
LANES = 128
ROWS = 8
GROUP = 128


def build_kernel(
    place_ref, occupation_ref, inverse_ref, orbitals_ref, hop_ref, energy_ref,
    derivs_ref, energy_derivs_ref,
    high_ref, low_ref, sites_ref, rows_ref, wide_ref, table_ref, first_ref, second_ref,
):
    electrons, walkers = occupation_ref.shape
    sites, orbitals = orbitals_ref.shape
    params = derivs_ref.shape[0]
    halves = walkers // LANES
    tiles = orbitals // ROWS

    for half in range(halves):
        for row in range(electrons * electrons):
            wide_ref[half, row] = jnp.broadcast_to(
                inverse_ref[row : row + 1, half * LANES : (half + 1) * LANES], (ROWS, LANES)
            )
    for number, source in enumerate((orbitals_ref, hop_ref)):
        for column in range(0, orbitals, LANES):
            turned = source[:, column : column + LANES].T
            high = turned.astype(jnp.bfloat16)
            where = pl.ds(number * orbitals + column, LANES)
            high_ref[where, :] = high
            low_ref[where, :] = (turned - high.astype(jnp.float32)).astype(jnp.bfloat16)

    def pick(electron, carry):
        occupied = occupation_ref[pl.ds(electron, 1), :]
        index = lax.broadcasted_iota(jnp.int32, (sites, walkers), 0)
        sites_ref[...] = jnp.where(index == occupied, 1.0, 0.0).astype(jnp.bfloat16)
        for row in range(0, 2 * orbitals, 256):
            where = pl.ds(row, 256)
            rows_ref[electron, where, :] = jnp.dot(
                high_ref[where, :], sites_ref[...], preferred_element_type=jnp.float32
            ) + jnp.dot(low_ref[where, :], sites_ref[...], preferred_element_type=jnp.float32)
        return carry

    lax.fori_loop(0, electrons, pick, 0)

    def contract(tile, carry):
        for half in range(halves):
            lanes = slice(half * LANES, (half + 1) * LANES)
            plain = [rows_ref[k, pl.ds(pl.multiple_of(tile * ROWS, ROWS), ROWS), lanes] for k in range(electrons)]
            hopped = [
                rows_ref[k, pl.ds(pl.multiple_of(orbitals + tile * ROWS, ROWS), ROWS), lanes]
                for k in range(electrons)
            ]
            scale = energy_ref[0:1, lanes] * 0.5
            for i in range(electrons):
                weight = wide_ref[half, i * electrons]
                ratio = weight * plain[0]
                energy = weight * hopped[0]
                for k in range(1, electrons):
                    weight = wide_ref[half, i * electrons + k]
                    ratio += weight * plain[k]
                    energy += weight * hopped[k]
                base = pl.multiple_of((i * tiles + tile) * 4 * ROWS, ROWS)
                table_ref[pl.ds(base + half, ROWS, stride=4), :] = ratio
                table_ref[pl.ds(base + 2 + half, ROWS, stride=4), :] = energy + scale * ratio
        return carry

    lax.fori_loop(0, tiles, contract, 0)

    def turned(value):
        return jnp.concatenate([value[2:4], value[0:2]])

    def pairs(group, carry):
        for j in range(GROUP):

            def take(which):
                return table_ref[pl.ds(pl.multiple_of(place_ref[which * params + group * GROUP + j], 4), 4), :]

            ia, jb, ib, ja = (take(which) for which in range(4))
            spot = pl.ds(4 * j, 4)
            first_ref[spot, :] = ia * jb - ib * ja
            second_ref[spot, :] = ia * turned(jb) - ib * turned(ja)
        for source, target, parts in ((first_ref, derivs_ref, 1), (second_ref, energy_derivs_ref, 2)):
            for row in range(0, GROUP, 2 * ROWS):
                for half in range(2):
                    value = source[pl.ds(row * 4 + half, 2 * ROWS, stride=4), :]
                    if parts == 2:
                        value = value + source[pl.ds(row * 4 + 2 + half, 2 * ROWS, stride=4), :]
                    target[
                        pl.ds(pl.multiple_of(group * GROUP + row, 2 * ROWS), 2 * ROWS),
                        half * LANES : (half + 1) * LANES,
                    ] = value.astype(jnp.bfloat16)
        return carry

    lax.fori_loop(0, params // GROUP, pairs, 0)


def build(occupation, inverse_slater, orbitals, hop_orbitals, local_energy, excitations):
    electrons, walkers = occupation.shape
    sites, orbital_count = orbitals.shape
    params = excitations.shape[1]

    electron_rows = excitations[:2] * (4 * orbital_count)
    orbital_rows = excitations[2:] * 4
    places = jnp.concatenate(
        [electron_rows + orbital_rows, electron_rows + orbital_rows[::-1]]
    ).reshape(-1)
    vmem = pl.BlockSpec(memory_space=pltpu.VMEM)
    return pl.pallas_call(
        build_kernel,
        out_shape=[jax.ShapeDtypeStruct((params, walkers), jnp.bfloat16)] * 2,
        in_specs=[pl.BlockSpec(memory_space=pltpu.SMEM)] + [vmem] * 5,
        out_specs=[vmem] * 2,
        scratch_shapes=[
            pltpu.VMEM((2 * orbital_count, sites), jnp.bfloat16),
            pltpu.VMEM((2 * orbital_count, sites), jnp.bfloat16),
            pltpu.VMEM((sites, walkers), jnp.bfloat16),
            pltpu.VMEM((electrons, 2 * orbital_count, walkers), jnp.float32),
            pltpu.VMEM((walkers // LANES, electrons * electrons, ROWS, LANES), jnp.float32),
            pltpu.VMEM((electrons * orbital_count * 4, LANES), jnp.float32),
            pltpu.VMEM((GROUP * 4, LANES), jnp.float32),
            pltpu.VMEM((GROUP * 4, LANES), jnp.float32),
        ],
        compiler_params=pltpu.CompilerParams(vmem_limit_bytes=49 * 1024 * 1024),
    )(
        places,
        occupation,
        inverse_slater.reshape(electrons * electrons, walkers),
        orbitals,
        hop_orbitals,
        local_energy[None],
    )

def walker_sums(derivs, energy_derivs):
    wide = derivs.astype(jnp.float32)
    return jnp.stack(
        [
            jnp.sum(wide, axis=1),
            jnp.sum(wide * wide, axis=1),
            jnp.sum(energy_derivs.astype(jnp.float32), axis=1),
        ]
    )


def dot_nt(left, right):
    return lax.dot_general(
        left, right, (((1,), (1,)), ((), ())), precision=HIGHEST, preferred_element_type=jnp.float32
    )


def dot_nn(left, right):
    return jnp.dot(left, right, precision=HIGHEST, preferred_element_type=jnp.float32)


def exchange(parts, axis):
    return lax.all_to_all(parts, axis, 0, 0)


def in_thirds(values):
    high = values.astype(jnp.bfloat16).astype(jnp.float32)
    rest = values - high
    middle = rest.astype(jnp.bfloat16).astype(jnp.float32)
    return high, middle, rest - middle


def lanes_of(shape):
    return lax.broadcasted_iota(jnp.int32, shape, 1)


def eliminate(matrix, right, full):
    count = matrix.shape[0]
    row = lax.broadcasted_iota(jnp.int32, (count, 1), 0)
    for j in range(count):
        pivot = matrix[j : j + 1, j : j + 1]
        scale = matrix[:, j : j + 1] / pivot
        keep = (row != j) if full else (row > j)
        scale = jnp.where(keep, scale, 0.0)
        right = right - scale * right[j : j + 1, :]
        matrix = matrix - scale * matrix[j : j + 1, :]
    diagonal = lanes_of(matrix.shape) == lax.broadcasted_iota(jnp.int32, matrix.shape, 0)
    return right, jnp.sum(jnp.where(diagonal, matrix, 0.0), axis=1, keepdims=True)


def advance_kernel(step, share, last, *refs):
    if last:
        got_ref, own_ref, state_ref, cents_ref = refs[:4]
        rows_refs = refs[4 : 4 + step]
        tail_ref, grams_ref, sent_ref = refs[4 + step :]
    elif step:
        got_ref, own_ref, state_ref, cents_ref, derivs_ref = refs[:5]
        block_ref, tail_ref, grams_ref, rows_ref, sent_ref = refs[5:]
    else:
        got_ref, own_ref, sums_ref, derivs_ref = refs[:4]
        block_ref, tail_ref, grams_ref, rows_ref, sent_ref = refs[4:]
    sources, _, width = got_ref.shape
    walkers = width - LANES
    owned = own_ref.shape[1]
    count = own_ref.shape[0]
    total = got_ref[0].astype(jnp.float32)
    for source in range(1, sources):
        total += got_ref[source].astype(jnp.float32)
    part = total[:, walkers:]
    grams = part[:count] + part[count:] + pltpu.roll(part[:count], LANES // 2, 1)
    lane = lanes_of((count, LANES))
    row = lax.broadcasted_iota(jnp.int32, (count, LANES), 0)
    identity = jnp.where(lane == row + LANES // 2, 1.0, 0.0)
    grams = jnp.where(lane < LANES // 2, grams, 0.0)
    grams_ref[...] = grams
    earlier = count * step
    if step:
        tail = jnp.where(lane < 2, pltpu.roll(grams, LANES - (earlier + count), 1), 0.0) + identity
    else:
        tail = identity
    right = jnp.concatenate([own_ref[...], total[:count, :walkers], total[count:, :walkers], tail], axis=1)
    gram = grams
    if step:
        overlap = grams[:, :earlier]
        right = right - dot_nn(overlap, jnp.concatenate([state_ref[...], cents_ref[...]], axis=1))
        gram = pltpu.roll(grams, LANES - earlier, 1)
        padded = jnp.concatenate([overlap, jnp.zeros((LANES - count, earlier), jnp.float32)])
        gram = gram - dot_nt(overlap, padded)
    right, pivots = eliminate(gram, right, False)
    right = right * lax.rsqrt(pivots)
    plain = right[:, owned : owned + walkers]
    energy = right[:, owned + walkers : owned + 2 * walkers]
    if not last:
        block_ref[...] = right[:, : owned + 2 * walkers]
    tail = right[:, owned + 2 * walkers :]
    if step:
        centers = [tail[:, 0:1], tail[:, 1:2]]
    else:
        centers = [jnp.mean(plain, axis=1, keepdims=True), jnp.mean(energy, axis=1, keepdims=True)]
        tail = jnp.where(lane == 0, centers[0], jnp.where(lane == 1, centers[1], tail))
    tail_ref[...] = tail
    center = jnp.concatenate(centers)
    rows = (jnp.concatenate([plain, energy]) - center).astype(jnp.bfloat16)
    wide = rows.astype(jnp.float32)
    if last:
        lefts = jnp.concatenate([state_ref[:, owned : owned + walkers], plain])
        every = [ref[...] for ref in rows_refs] + [wide]
        rights = [value[:count] for value in every] + [value[count:] for value in every]
        size = 2 * count * len(every)
        rights = jnp.concatenate(rights + [jnp.zeros((LANES - size, walkers), jnp.float32)])
        products = dot_nt(lefts, rights)
        for owner in range(sent_ref.shape[0]):
            sent_ref[owner] = products
        return
    rows_ref[...] = wide
    filled = jnp.concatenate([plain, jnp.zeros((LANES - count, walkers), jnp.float32)])
    if step:
        high, middle, low = in_thirds(dot_nt(wide, filled))
        inner = (high + pltpu.roll(middle, 32, 1) + pltpu.roll(low, 64, 1)).astype(jnp.bfloat16)
    else:
        inner = dot_nt(wide + center, filled)
        inner = inner + jnp.where(lanes_of(inner.shape) == count, walkers * center, 0.0)
        across = dot_nt(jnp.ones((count, walkers), jnp.float32), filled)
    for owner in range(sent_ref.shape[0]):
        where = slice(owner * share, (owner + 1) * share)
        back = lax.dot_general(
            rows, derivs_ref[where, :], (((1,), (1,)), ((), ())), preferred_element_type=jnp.float32
        )
        if step:
            sent_ref[owner, :, :share] = back.astype(jnp.bfloat16)
            sent_ref[owner, :, share:] = inner
        else:
            sent_ref[owner, : 2 * count, :share] = back + center * sums_ref[0:1, where]
            sent_ref[owner, : 2 * count, share:] = inner
            sent_ref[owner, 2 * count :, :share] = sums_ref[:, where]
            sent_ref[owner, 2 * count :, share:] = across


def correct_kernel(step, walkers, *refs):
    if step:
        got_ref, state_ref, stats_ref, own_ref, sent_ref, stack_ref = refs
    else:
        got_ref, state_ref, own_ref, sent_ref, stats_ref, cents_ref, stack_ref = refs
    sources, _, width = got_ref.shape
    owned = width - LANES
    count = own_ref.shape[0]
    earlier = count * (step + 1)
    total = got_ref[0].astype(jnp.float32)
    for source in range(1, sources):
        total += got_ref[source].astype(jnp.float32)
    total = total * (1.0 / walkers)
    images = total[: 2 * count, :owned]
    inner = total[: 2 * count, owned:]
    if step:
        inner = inner + pltpu.roll(inner, LANES - 32, 1) + pltpu.roll(inner, LANES - 64, 1)
        stats = stats_ref[...]
    else:
        mean_o = total[2 * count : 2 * count + 1, :owned]
        mean_h = total[2 * count + 2 : 2 * count + 3, :owned]
        square = total[2 * count + 1 : 2 * count + 2, :owned]
        kind = lax.broadcasted_iota(jnp.int32, (count, owned), 0)
        diagonal = square - mean_o * mean_o + EPS_SHIFT
        stats = jnp.where(
            kind == 0, mean_o, jnp.where(kind == 1, mean_h, jnp.where(kind == 2, diagonal, 0.0))
        )
        stats_ref[...] = stats
        center = inner[:, count : count + 1]
        inner = inner - center * total[2 * count : 2 * count + 1, owned:]
        images = images - center * mean_o
        lane = lanes_of((count, LANES))
        cents_ref[...] = jnp.where(
            lane == 0, center[:count], jnp.where(lane == 1, center[count:], 0.0)
        )
    block = state_ref[earlier - count :, :owned]
    lane = lanes_of((count, LANES))
    unit = jnp.where(lane == lax.broadcasted_iota(jnp.int32, lane.shape, 0), 1.0, 0.0)
    a_matrix = jnp.where(lane < count, inner[:count], 0.0) + EPS_SHIFT * unit
    turned_b = inner[count:] + ENERGY_SHIFT * unit
    s_image = images[:count] + EPS_SHIFT * block
    h_image = images[count:] + ENERGY_SHIFT * block
    solved, pivots = eliminate(a_matrix, s_image, True)
    solved = solved / pivots
    correction = h_image - dot_nn(turned_b[:, :count], solved)
    correction = correction / stats[2:3, :]
    own_ref[...] = correction
    stack_ref[...] = jnp.zeros_like(stack_ref)
    stack_ref[:earlier, :] = state_ref[:, :owned]
    stack_ref[earlier : earlier + count, :] = correction
    stack_ref[earlier + count : earlier + 2 * count, :] = stats
    grams = dot_nt(correction, stack_ref[...])
    for target in range(sent_ref.shape[0]):
        sent_ref[target, :, :owned] = correction
        sent_ref[target, :, owned:] = grams


def project_kernel(first, got_ref, derivs_ref, energy_ref, sent_ref):
    params = derivs_ref.shape[0]
    if first:
        count, sources, owned = got_ref.shape[0], 1, params
    else:
        sources, count, width = got_ref.shape
        owned = width - LANES
    grams = jnp.zeros((count, LANES), jnp.float32)
    plain = energy = None
    for source in range(sources):
        if first:
            values = got_ref[...]
            grams = jnp.concatenate(
                [dot_nt(values, values), jnp.zeros((count, LANES - count), jnp.float32)], axis=1
            )
        else:
            values = got_ref[source, :, :owned]
            grams += got_ref[source, :, owned:]
        high = values.astype(jnp.bfloat16).astype(jnp.float32)
        both = jnp.concatenate([high, values - high]).astype(jnp.bfloat16)
        more = [
            jnp.dot(
                both,
                table[source * owned : (source + 1) * owned, :],
                preferred_element_type=jnp.float32,
            )
            for table in (derivs_ref, energy_ref)
        ]
        plain, energy = more if plain is None else (plain + more[0], energy + more[1])
    images = jnp.concatenate([plain[:count] + plain[count:], energy[:count] + energy[count:]])
    images = images.astype(jnp.bfloat16)
    high, middle, low = in_thirds(jnp.where(lanes_of(grams.shape) < LANES // 2, grams, 0.0))
    side = jnp.concatenate([high + pltpu.roll(low, LANES // 2, 1), middle]).astype(jnp.bfloat16)
    walkers = images.shape[1]
    for target in range(sent_ref.shape[0]):
        sent_ref[target, :, :walkers] = images
        sent_ref[target, :, walkers:] = side


def finish_kernel(walkers, got_ref, first_ref, second_ref):
    total = got_ref[0]
    for source in range(1, got_ref.shape[0]):
        total += got_ref[source]
    total = total * (1.0 / walkers)
    size = first_ref.shape[0]
    unit = jnp.where(lanes_of(total.shape) == lax.broadcasted_iota(jnp.int32, total.shape, 0), 1.0, 0.0)
    first_ref[...] = (pltpu.roll(total, LANES - size, 1) + ENERGY_SHIFT * unit)[:, :size]
    second_ref[...] = (total + EPS_SHIFT * unit)[:, :size]


def stage(body, outs, args, scratch=()):
    vmem = pl.BlockSpec(memory_space=pltpu.VMEM)
    return pl.pallas_call(
        body,
        out_shape=[jax.ShapeDtypeStruct(shape, dtype) for shape, dtype in outs],
        in_specs=[vmem] * len(args),
        out_specs=[vmem] * len(outs),
        scratch_shapes=list(scratch),
        compiler_params=pltpu.CompilerParams(vmem_limit_bytes=20 * 1024 * 1024),
    )(*args)


def on_device(
    occupation, inverse_slater, orbitals, hop_orbitals, local_energy, excitations, initial_block
):
    walker_devices = lax.axis_size("walker")
    param_devices = lax.axis_size("param")
    local_walkers = local_energy.shape[0]
    walkers = local_walkers * walker_devices
    block_rows = excitations.shape[1]
    count = initial_block.shape[1]
    params = block_rows * param_devices
    owned = block_rows // walker_devices
    f32, bf16 = jnp.float32, jnp.bfloat16
    derivs, energy_derivs = build(
        occupation, inverse_slater, orbitals, hop_orbitals, local_energy, excitations
    )
    sums = walker_sums(derivs, energy_derivs)
    sums = jnp.pad(sums, ((0, count - sums.shape[0]), (0, 0)))
    start = initial_block.T
    offset = lax.axis_index("walker") * owned
    own = lax.dynamic_slice_in_dim(start, offset, owned, 1)
    state = cents = stats = None
    wholes, rows = [], []
    for step in range(ITERS + 1):
        if step:
            pieces = exchange(sent, "walker")
        (sent,) = stage(
            functools.partial(project_kernel, step == 0),
            [((param_devices, 2 * count, local_walkers + LANES), bf16)],
            (pieces if step else start, derivs, energy_derivs),
        )
        got = exchange(sent, "param")
        last = step == ITERS
        body = functools.partial(advance_kernel, step, owned, last)
        if last:
            tail, grams, sent = stage(
                body,
                [
                    ((count, LANES), f32),
                    ((count, LANES), f32),
                    ((walker_devices, count * (ITERS + 1), LANES), f32),
                ],
                (got, own, state, cents, *rows),
            )
        else:
            outs = [
                ((count, owned + 2 * local_walkers), f32),
                ((count, LANES), f32),
                ((count, LANES), f32),
                ((2 * count, local_walkers), f32),
                ((walker_devices, 2 * count, owned + LANES), bf16)
                if step
                else ((walker_devices, 3 * count, owned + LANES), f32),
            ]
            block, tail, grams, wide, sent = stage(
                body, outs, (got, own, state, cents, derivs) if step else (got, own, sums, derivs)
            )
        whole = start
        if step:
            whole = pieces[:, :, :owned].transpose(1, 0, 2).reshape(count, block_rows)
            whole = whole - dot_nn(grams[:, : count * step], jnp.concatenate(wholes))
        wholes.append(dot_nn(tail[:, LANES // 2 : LANES // 2 + count], whole))
        if last:
            break
        rows.append(wide)
        state = block if step == 0 else jnp.concatenate([state, block])
        got = exchange(sent, "walker")
        outs = [
            ((count, owned), f32),
            ((walker_devices, count, owned + LANES), f32),
        ]
        scratch = [pltpu.VMEM((LANES, owned), f32)]
        if step:
            own, sent = stage(
                functools.partial(correct_kernel, step, walkers), outs, (got, state, stats), scratch
            )
            cents = jnp.concatenate(
                [cents, jnp.where(jnp.arange(LANES) < 2, tail, 0.0)]
            )
        else:
            outs += [((count, owned), f32), ((count, LANES), f32)]
            own, sent, stats, cents = stage(
                functools.partial(correct_kernel, step, walkers), outs, (got, state), scratch
            )
            shift = tail[:, :2] - cents[:, :2]
            rows[0] = wide + shift.T.reshape(2 * count, 1)
    size = count * (ITERS + 1)
    proj_h, proj_s = stage(
        functools.partial(finish_kernel, walkers),
        [((size, size), f32)] * 2,
        (exchange(sent, "walker"),),
    )
    return (math.sqrt(params) * jnp.concatenate(wholes).T, proj_h, proj_s)


def solution(mesh):
    placed = (
        P(None, "walker"),
        P(None, None, "walker"),
        P(),
        P(),
        P("walker"),
        P(None, "param"),
        P("param", None),
    )
    return jax.shard_map(
        on_device,
        mesh=mesh,
        in_specs=placed,
        out_specs=(P("param", None), P(), P()),
        check_vma=False,
    )
```
